256 devices in a mesh: dp: 4 (over z_hi, core), chan: 4 (over x), space: 16 (over z_lo, y).
Axes of the slice: x: 4, y: 4, z: 8 (z_hi: 2, z_lo: 4; z = z_hi * 4 + z_lo), core: 2. Of those that a mesh axis runs over, the one named last changes fastest.
Arguments:
- section_input: bfloat16 [4, 2, 128, 128, 512], P('dp', None, 'space', None, 'chan'), may hold values from -6 to 6
- middle: bfloat16 [4, 2, 128, 128, 512], P('dp', None, 'space', None, 'chan'), may hold values from -6 to 6
- out_grad: bfloat16 [4, 2, 128, 128, 512], P('dp', None, 'space', None, 'chan'), may hold values from -6 to 6
- kernels: bfloat16 [2, 3, 3, 512, 512], P(None, None, None, None, 'chan'), may hold values from -0.09375 to 0.09375
- master: float32 [2, 3, 3, 512, 512], P(None, None, None, ('dp', 'space'), 'chan'), may hold values from -0.09375 to 0.09375
- moment: float32 [2, 3, 3, 512, 512], P(None, None, None, ('dp', 'space'), 'chan'), may hold values from -600 to 600
- second: float32 [2, 3, 3, 512, 512], P(None, None, None, ('dp', 'space'), 'chan'), may hold values from 1000 to 100000
Outputs:
- input_grad: bfloat16 [4, 2, 128, 128, 512], P('dp', None, 'space', None, 'chan')
- new_kernels: bfloat16 [2, 3, 3, 512, 512], P(None, None, None, None, 'chan')
- new_master: float32 [2, 3, 3, 512, 512], P(None, None, None, ('dp', 'space'), 'chan')
- new_moment: float32 [2, 3, 3, 512, 512], P(None, None, None, ('dp', 'space'), 'chan')
- new_second: float32 [2, 3, 3, 512, 512], P(None, None, None, ('dp', 'space'), 'chan')
The draws below stay inside these ranges and needn't reach their ends.
All inputs are finite; a program needn't handle non-finite values.
Results may differ from the reference program's by a relative error of at most 0.0015.
The reference program's roundings to bfloat16 on the way (of `act2`, `mid_grad` and `act1`) count: a program that leaves them out, or rounds other values in their place, can miss the bound.
Values may be sent and summed in bfloat16 or wider, within the bound.
A program may use at most 128 MiB of HBM per device.

```python
import math
import jax
import jax.numpy as jnp

C = 512
WIDTH = 128
FRAMES = 2
CLIPS = 4
HEIGHT = 128


def steps_of(own_key, dims, split, smallest, high):
    def one(dim, parts):
        draws = jax.random.uniform(jax.random.fold_in(jax.random.fold_in(own_key, 6), dim), (parts,), jnp.float32, smallest / len(split), high / len(split))
        return jnp.repeat(jnp.exp(draws), dims[dim] // parts).reshape((-1,) + (1,) * (len(dims) - dim - 1))

    factor_of = one(*split[0])
    for cut in split[1:]:
        factor_of = factor_of * one(*cut)
    return factor_of


def normal_values(own_key, shape, spread, bound, pieces=(), dtype=jnp.bfloat16):
    result = spread * jax.random.normal(own_key, shape, jnp.float32)
    if pieces:
        result = result * steps_of(own_key, shape, pieces, -0.22, 0.18)
    return jnp.clip(result, -bound, bound).astype(dtype)


def setup_inputs(seed: int = 0) -> dict:
    keys = jax.random.split(jax.random.key(seed), 8)
    section_input = normal_values(keys[0], (CLIPS, FRAMES, HEIGHT, WIDTH, C), 1.0, 6.0, ((0, 4), (2, 16), (4, 4)))
    middle = normal_values(keys[1], (CLIPS, FRAMES, HEIGHT, WIDTH, C), 1.0, 6.0, ((0, 4), (2, 16), (4, 4)))
    out_grad = normal_values(keys[2], (CLIPS, FRAMES, HEIGHT, WIDTH, C), 1.0, 6.0, ((0, 4), (2, 16), (4, 4)))
    kernels = normal_values(keys[3], (2, 3, 3, C, C), (9 * C) ** -0.5, 0.09375, ((4, 4),))
    master = normal_values(keys[4], (2, 3, 3, C, C), (9 * C) ** -0.5, 0.09375, ((3, 64), (4, 4)), jnp.float32)
    moment = normal_values(keys[5], (2, 3, 3, C, C), 100.0, 600.0, ((3, 64), (4, 4)), jnp.float32)
    second = jnp.clip(jnp.exp(math.log(100000.0) - 4.6051702 * jax.random.uniform(keys[6], (2, 3, 3, C, C), jnp.float32) ** steps_of(keys[6], (2, 3, 3, C, C), ((3, 64), (4, 4)), -0.2, 0.2)), 1000.0, 100000.0)
    return {"section_input": section_input, "middle": middle, "out_grad": out_grad, "kernels": kernels, "master": master, "moment": moment, "second": second}


def dsilu(value):
    sig = jax.nn.sigmoid(value)
    return sig * (1.0 + value * (1.0 - sig))

def conv_back(act, grad, weight):
    padded = jnp.pad(grad, ((0, 0), (0, 0), (1, 1), (1, 1), (0, 0)))
    rows = grad.shape[2]
    cols = grad.shape[3]
    flat = act.reshape(-1, C)
    kernel_list = []
    partial_value = jnp.zeros((flat.shape[0], C), jnp.float32)
    for row_tap in range(3):
        for col_tap in range(3):
            view = padded[:, :, 2 - row_tap:2 - row_tap + rows, 2 - col_tap:2 - col_tap + cols, :].reshape(-1, C)
            kernel_list.append(jnp.dot(flat.T, view, preferred_element_type=jnp.float32))
            partial_value = partial_value + jnp.dot(view, weight[row_tap, col_tap].T, preferred_element_type=jnp.float32)
    return (jnp.stack(kernel_list).reshape(3, 3, C, C), partial_value.reshape(grad.shape))

def reference(section_input, middle, out_grad, kernels, master, moment, second):
    mid_f = middle.astype(jnp.float32)
    in_f = section_input.astype(jnp.float32)
    act2 = jax.nn.silu(mid_f).astype(jnp.bfloat16)
    grad2, back2 = conv_back(act2, out_grad, kernels[1])
    mid_grad = (back2 * dsilu(mid_f)).astype(jnp.bfloat16)
    act1 = jax.nn.silu(in_f).astype(jnp.bfloat16)
    grad1, back1 = conv_back(act1, mid_grad, kernels[0])
    input_grad = (out_grad.astype(jnp.float32) + back1 * dsilu(in_f)).astype(jnp.bfloat16)
    grads = jnp.stack([grad1, grad2])
    new_moment = 0.9 * moment + 0.1 * grads
    new_second = 0.999 * second + 0.001 * grads * grads
    corrected = new_moment / (1.0 - 0.9 ** 10)
    scale_term = jnp.sqrt(new_second / (1.0 - 0.999 ** 10)) + 1e-08
    new_master = master - 0.01 * corrected / scale_term
    return (input_grad, new_master.astype(jnp.bfloat16), new_master, new_moment, new_second)
```

```python
import jax
import jax.numpy as jnp
from jax import lax
from jax.experimental import pallas as pl
from jax.experimental.pallas import tpu as pltpu
from jax.sharding import PartitionSpec as P

BF = jnp.bfloat16
F32 = jnp.float32
MESH = pl.DeviceIdType.MESH
PX = 1024
SLAB = 80
VMEM_LIMIT = 56 * 1024 * 1024


def sigmoid(v):
    return 1.0 / (1.0 + jnp.exp(-v))


def dsilu(v):
    sig = sigmoid(v)
    return sig * (1.0 + v * (1.0 - sig))


def nt_dot(a, b):
    return lax.dot_general(a, b, (((1,), (1,)), ((), ())), preferred_element_type=F32)


class Sems:
    def __init__(self, ref):
        self.ref = ref
        self.used = 0

    def take(self, count=1):
        base = self.used
        self.used += count
        return base


def kernel(
    x_in, mid_in, og_in, kern, master, moment, second,
    ig_out, slab_out, master_out, moment_out, second_out,
    xpad, midpad, gog, gmg, w, actt, red, back, halo_in, halo_out, core_in,
    ysend, yrecv, zsend, zrecv, perm_src, perm_dst, adam_in, adam_out, slabs, ig_buf, sems,
):
    chan = lax.axis_index("chan")
    dp = lax.axis_index("dp")
    space = lax.axis_index("space")
    z_hi, core = dp // 2, dp % 2
    z_lo, y = space // 4, space % 4
    z = z_hi * 4 + z_lo
    pool = Sems(sems)
    sends = []

    def at_chan(p):
        return {"chan": (chan + p) % 4}

    def at_y(p):
        return {"space": z_lo * 4 + (y + p) % 4}

    def at_z(p):
        other = (z + p) % 8
        return {"dp": (other // 4) * 2 + core, "space": (other % 4) * 4 + y}

    sibling = {"dp": z_hi * 2 + (1 - core)}
    mirror = {"dp": chan, "chan": dp}
    has_prev = space > 0
    has_next = space < 15
    crosses = chan != dp

    def send(src, dst, target, recv_sem, when=None):
        copy = pltpu.make_async_remote_copy(
            src_ref=src, dst_ref=dst, send_sem=sems.at[pool.take()], recv_sem=sems.at[recv_sem],
            device_id=target, device_id_type=MESH,
        )
        if when is None:
            copy.start()
        else:
            pl.when(when)(copy.start)
        sends.append((copy, when))

    def wait_in(dst, sem):
        pltpu.make_async_copy(dst, dst, sems.at[sem]).wait()

    def load(src, dst):
        copy = pltpu.make_async_copy(src, dst, sems.at[pool.take()])
        copy.start()
        return copy

    inside = pl.ds(128, PX)
    load_mid = load(mid_in, midpad.at[:, inside, :])
    load_x = load(x_in, xpad.at[:, inside, :])
    load_og = load(og_in, gog.at[:, inside, pl.ds(0, 128)])
    my_rows = pl.ds(core * 64 + y * 16, 16)
    load_w = [
        load(kern.at[l, :, pl.ds(chan * 128 + core * 64 + y * 16, 16), :], w.at[l, :, my_rows, pl.ds(0, 128)])
        for l in range(2)
    ]
    load_adam = [load(ref, adam_in.at[k]) for k, ref in enumerate((master, moment, second))]

    barrier = pltpu.get_barrier_semaphore()

    def greet(target):
        pl.semaphore_signal(barrier, inc=1, device_id=target, device_id_type=MESH)

    for p in range(1, 4):
        greet(at_chan(p))
        greet(at_y(p))
    for p in range(1, 8):
        greet(at_z(p))
    greet(sibling)
    prev, nxt = {"space": space - 1}, {"space": space + 1}
    pl.when(has_prev)(lambda: greet(prev))
    pl.when(has_next)(lambda: greet(nxt))
    pl.when(crosses)(lambda: greet(mirror))

    zero_row = jnp.zeros((128, 512), BF)
    for g in (gog, gmg):
        for f in range(2):
            g[f, pl.ds(0, 128), :] = zero_row
            g[f, pl.ds(128 + PX, 128), :] = zero_row

    @pl.when(space == 0)
    def _():
        for pad in (midpad, xpad):
            pad[:, pl.ds(0, 128), :] = jnp.zeros((2, 128, 128), BF)

    @pl.when(space == 15)
    def _():
        for pad in (midpad, xpad):
            pad[:, pl.ds(128 + PX, 128), :] = jnp.zeros((2, 128, 128), BF)

    expected = 14 + has_prev.astype(jnp.int32) + has_next.astype(jnp.int32) + crosses.astype(jnp.int32)
    pl.semaphore_wait(barrier, expected)

    gathers = {}

    def half(f, h):
        return (f, pl.ds(128 + 512 * h, 512))

    def gather_own(name, g, src, f):
        sem = gathers.setdefault(name, {})
        for k in ("left", "right", "far"):
            for h in range(2):
                sem[k, f, h] = pool.take()
        for step in range(2):
            h = step
            send(src(f, h), g.at[(*half(f, h), pl.ds(128, 128))], at_chan(1), sem["left", f, h])
            h = 1 - step
            send(src(f, h), g.at[(*half(f, h), pl.ds(384, 128))], at_chan(3), sem["right", f, h])

    def gather_forward(name, g, f):
        sem = gathers[name]
        here = g.at[(*half(f, 0), pl.ds(128, 128))]
        wait_in(here, sem["left", f, 0])
        send(here, g.at[(*half(f, 0), pl.ds(256, 128))], at_chan(1), sem["far", f, 0])
        here = g.at[(*half(f, 1), pl.ds(384, 128))]
        wait_in(here, sem["right", f, 1])
        send(here, g.at[(*half(f, 1), pl.ds(256, 128))], at_chan(3), sem["far", f, 1])

    def gather_wait(name, g, f):
        sem = gathers[name]
        wait_in(g.at[(*half(f, 1), pl.ds(128, 128))], sem["left", f, 1])
        wait_in(g.at[(*half(f, 0), pl.ds(384, 128))], sem["right", f, 0])
        for h in range(2):
            wait_in(g.at[(*half(f, h), pl.ds(256, 128))], sem["far", f, h])

    w_sem = {}

    def weights_chan(l):
        for p in range(1, 4):
            w_sem["x", l, p] = pool.take()
            their = (chan + p) % 4
            send(
                kern.at[l, :, pl.ds(their * 128 + core * 64 + y * 16, 16), :],
                w.at[l, :, my_rows, pl.ds(128 * p, 128)],
                at_chan(p), w_sem["x", l, p],
            )

    def weights_y(l):
        load_w[l].wait()
        for p in range(1, 4):
            wait_in(w.at[l, :, my_rows, pl.ds(128 * p, 128)], w_sem["x", l, p])
        for p in range(1, 4):
            w_sem["y", l, p] = pool.take()
            here = w.at[l, :, my_rows, :]
            send(here, here, at_y(p), w_sem["y", l, p])

    def weights_core(l):
        for p in range(1, 4):
            wait_in(w.at[l, :, pl.ds(core * 64 + ((y + 4 - p) % 4) * 16, 16), :], w_sem["y", l, p])
        w_sem["core", l] = pool.take()
        here = w.at[l, :, pl.ds(core * 64, 64), :]
        send(here, here, sibling, w_sem["core", l])

    def weights_wait(l):
        wait_in(w.at[l, :, pl.ds((1 - core) * 64, 64), :], w_sem["core", l])

    rim_sem = {}

    def rims(k, src, pad):
        up, down = pool.take(), pool.take()
        rim_sem[k] = (up, down)
        send(src.at[:, pl.ds(PX - 128, 128), :], pad.at[:, pl.ds(0, 128), :], nxt, up, has_next)
        send(src.at[:, pl.ds(0, 128), :], pad.at[:, pl.ds(128 + PX, 128), :], prev, down, has_prev)

    def rims_wait(k, pad):
        up, down = rim_sem[k]
        pl.when(has_prev)(lambda: wait_in(pad.at[:, pl.ds(0, 128), :], up))
        pl.when(has_next)(lambda: wait_in(pad.at[:, pl.ds(128 + PX, 128), :], down))

    def transpose_act(pad):
        lane = lax.broadcasted_iota(jnp.int32, (128, 128), 1)

        def body(i, carry):
            f, row = i // 10, i % 10
            v = pad[f, pl.ds(row * 128, 128), :].astype(F32)
            a = (v * sigmoid(v)).astype(BF).astype(F32).T
            at = pl.ds(pl.multiple_of(row * 128, 128), 128)
            before = jnp.where(lane == 0, 0.0, pltpu.roll(a, 1, 1))
            after = jnp.where(lane == 127, 0.0, pltpu.roll(a, 127, 1))
            actt[f, pl.ds(0, 128), at] = before.astype(BF)
            actt[f, pl.ds(128, 128), at] = a.astype(BF)
            actt[f, pl.ds(256, 128), at] = after.astype(BF)
            return carry

        lax.fori_loop(0, 20, body, 0)

    def kernel_grad(l, g, f):
        cotangent = g[f, inside, :]
        for r in range(3):
            part = jnp.dot(actt[f, :, pl.ds(128 * r, PX)], cotangent, preferred_element_type=F32)
            for k in range(4):
                block = part[:, 128 * k : 128 * k + 128].reshape(3, 128, 128)
                if f:
                    block = block + red[l, k, pl.ds(3 * r, 3)]
                red[l, k, pl.ds(3 * r, 3)] = block

    def weight_rows(l, r):
        return w[l, pl.ds(3 * r, 3)].reshape(384, 512)

    def join_taps(acc):
        rows = acc.shape[0]
        col = lax.broadcasted_iota(jnp.int32, (rows, 128), 0) % 128
        first = jnp.where(col == 127, 0.0, pltpu.roll(acc[:, 0:128], rows - 1, 0))
        last = jnp.where(col == 0, 0.0, pltpu.roll(acc[:, 256:384], 1, 0))
        return first + acc[:, 128:256] + last

    halo_sem = {}

    def back_halos(l, g, f):
        up, down = pool.take(), pool.take()
        halo_sem[l, f] = (up, down)
        halo_out[l, f, 0] = join_taps(nt_dot(g[f, pl.ds(128, 128), :], weight_rows(l, 0)))
        halo_out[l, f, 1] = join_taps(nt_dot(g[f, pl.ds(PX, 128), :], weight_rows(l, 2)))
        send(halo_out.at[l, f, 0], halo_in.at[l, f, 1], prev, down, has_prev)
        send(halo_out.at[l, f, 1], halo_in.at[l, f, 0], nxt, up, has_next)

    def back_rows(l, g, f):
        def body(i, carry):
            start = i * 256
            acc = jnp.zeros((256, 384), F32)
            for r in range(3):
                rows = pl.ds(pl.multiple_of(start + (2 - r) * 128, 128), 256)
                acc = acc + nt_dot(g[f, rows, :], weight_rows(l, r))
            back[pl.ds(pl.multiple_of(start, 128), 256), :] = join_taps(acc)
            return carry

        lax.fori_loop(0, 4, body, 0)

    def halos_add(l, f):
        up, down = halo_sem[l, f]

        @pl.when(has_prev)
        def _():
            wait_in(halo_in.at[l, f, 0], up)
            back[pl.ds(0, 128), :] = back[pl.ds(0, 128), :] + halo_in[l, f, 0]

        @pl.when(has_next)
        def _():
            wait_in(halo_in.at[l, f, 1], down)
            back[pl.ds(PX - 128, 128), :] = back[pl.ds(PX - 128, 128), :] + halo_in[l, f, 1]

    def middle_grad(f):
        def body(i, carry):
            rows = pl.ds(pl.multiple_of(i * 128, 128), 128)
            padded = pl.ds(pl.multiple_of(i * 128 + 128, 128), 128)
            v = midpad[f, padded, :].astype(F32)
            gmg[f, padded, pl.ds(0, 128)] = (back[rows, :] * dsilu(v)).astype(BF)
            return carry

        lax.fori_loop(0, 8, body, 0)

    def input_grad(f):
        def body(i, carry):
            rows = pl.ds(pl.multiple_of(i * 128, 128), 128)
            padded = pl.ds(pl.multiple_of(i * 128 + 128, 128), 128)
            v = xpad[f, padded, :].astype(F32)
            og = gog[f, padded, pl.ds(0, 128)].astype(F32)
            ig_buf[f, rows, :] = (og + back[rows, :] * dsilu(v)).astype(BF)
            return carry

        lax.fori_loop(0, 8, body, 0)

    r_sem = {}

    def slot_of(block):
        return (chan + 4 - block) % 4

    def reduce_core(l):
        for h in range(2):
            r_sem["core", l, h] = pool.take()
            send(red.at[l, slot_of(2 * h + 1 - core)], core_in.at[l, h], sibling, r_sem["core", l, h])

    def reduce_y(l):
        for h in range(2):
            wait_in(core_in.at[l, h], r_sem["core", l, h])
            k = slot_of(2 * h + core)

            def body(t, carry):
                total = (red[l, k, t] + core_in[l, h, t]).reshape(4, 4, 8, 128)
                for q in range(4):
                    ysend[l, q, h, t] = total[:, q].reshape(32, 128).astype(BF)
                return carry

            lax.fori_loop(0, 9, body, 0)
        for p in range(1, 4):
            r_sem["y", l, p] = pool.take()
            send(ysend.at[l, (y + p) % 4], yrecv.at[l, p - 1], at_y(p), r_sem["y", l, p])

    def reduce_z(l):
        for p in range(1, 4):
            wait_in(yrecv.at[l, p - 1], r_sem["y", l, p])

        def body(h, carry):
            total = ysend[l, y, h].astype(F32)
            for p in range(3):
                total = total + yrecv[l, p, h].astype(F32)
            total = total.reshape(9, 4, 8, 128)
            for q in range(4):
                rows = jnp.concatenate([total[:, q].reshape(72, 128), jnp.zeros((8, 128), F32)], axis=0)
                zsend[l, h * 4 + q] = rows.astype(BF)
            return carry

        lax.fori_loop(0, 2, body, 0)
        for p in range(1, 8):
            r_sem["z", l, p] = pool.take()
            send(zsend.at[l, (z + p) % 8], zrecv.at[l, p - 1], at_z(p), r_sem["z", l, p])

    def reduce_owner(l):
        for p in range(1, 8):
            wait_in(zrecv.at[l, p - 1], r_sem["z", l, p])
        total = zsend[l, z].astype(F32)
        for p in range(7):
            total = total + zrecv[l, p].astype(F32)
        perm_src[l] = total[0:72].reshape(9, 8, 128)
        r_sem["own", l] = pool.take()
        send(perm_src.at[l], perm_dst.at[l], mirror, r_sem["own", l], crosses)

        @pl.when(jnp.logical_not(crosses))
        def _():
            perm_dst[l] = perm_src[l]

    a_sem = {}

    def adam(l):
        if l == 1:
            for copy in load_adam:
                copy.wait()
        pl.when(crosses)(lambda: wait_in(perm_dst.at[l], r_sem["own", l]))
        grads = perm_dst[l]
        new_moment = 0.9 * adam_in[1, l] + 0.1 * grads
        new_second = 0.999 * adam_in[2, l] + 0.001 * grads * grads
        corrected = new_moment / (1.0 - 0.9**10)
        scale_term = jnp.sqrt(new_second / (1.0 - 0.999**10)) + 1e-08
        new_master = adam_in[0, l] - 0.01 * corrected / scale_term
        adam_out[0, l] = new_master
        adam_out[1, l] = new_moment
        adam_out[2, l] = new_second
        rows = jnp.concatenate([new_master.reshape(72, 128), jnp.zeros((8, 128), F32)], axis=0)
        slabs[l, dp, space] = rows.astype(BF)
        here = slabs.at[l, dp, space]
        for p in range(1, 8):
            a_sem["z", l, p] = pool.take()
            send(here, here, at_z(p), a_sem["z", l, p])

    def spread_y(l):
        for p in range(1, 8):
            other = (z + 8 - p) % 8
            wait_in(slabs.at[l, (other // 4) * 2 + core, (other % 4) * 4 + y], a_sem["z", l, p])
        for p in range(1, 4):
            for q in range(8):
                a_sem["y", l, p, q] = pool.take()
                here = slabs.at[l, (q // 4) * 2 + core, (q % 4) * 4 + y]
                send(here, here, at_y(p), a_sem["y", l, p, q])

    def spread_core(l):
        for p in range(1, 4):
            for q in range(8):
                other = (y + 4 - p) % 4
                wait_in(slabs.at[l, (q // 4) * 2 + core, (q % 4) * 4 + other], a_sem["y", l, p, q])
        for h in range(2):
            a_sem["core", l, h] = pool.take()
            here = slabs.at[l, h * 2 + core]
            send(here, here, sibling, a_sem["core", l, h])

    def spread_wait(l):
        for h in range(2):
            wait_in(slabs.at[l, h * 2 + 1 - core], a_sem["core", l, h])

    def og_half(f, h):
        return og_in.at[f, pl.ds(512 * h, 512), :]

    def mg_half(f, h):
        return gmg.at[(*half(f, h), pl.ds(0, 128))]

    weights_chan(1)
    gather_own("og", gog, og_half, 0)
    rims("mid", mid_in, midpad)
    rims("x", x_in, xpad)
    weights_y(1)
    gather_forward("og", gog, 0)
    weights_chan(0)
    gather_own("og", gog, og_half, 1)
    load_mid.wait()
    rims_wait("mid", midpad)
    transpose_act(midpad)
    weights_core(1)
    weights_y(0)
    gather_wait("og", gog, 0)
    load_og.wait()
    weights_wait(1)
    back_halos(1, gog, 0)
    back_rows(1, gog, 0)
    gather_forward("og", gog, 1)
    halos_add(1, 0)
    middle_grad(0)
    gather_own("mg", gmg, mg_half, 0)
    weights_core(0)
    kernel_grad(1, gog, 0)
    gather_wait("og", gog, 1)
    back_halos(1, gog, 1)
    back_rows(1, gog, 1)
    gather_forward("mg", gmg, 0)
    halos_add(1, 1)
    middle_grad(1)
    gather_own("mg", gmg, mg_half, 1)
    kernel_grad(1, gog, 1)
    reduce_core(1)
    load_x.wait()
    rims_wait("x", xpad)
    transpose_act(xpad)
    reduce_y(1)
    weights_wait(0)
    gather_wait("mg", gmg, 0)
    kernel_grad(0, gmg, 0)
    back_halos(0, gmg, 0)
    back_rows(0, gmg, 0)
    reduce_z(1)
    gather_forward("mg", gmg, 1)
    halos_add(0, 0)
    input_grad(0)
    reduce_owner(1)
    adam(1)
    gather_wait("mg", gmg, 1)
    kernel_grad(0, gmg, 1)
    reduce_core(0)
    spread_y(1)
    back_halos(0, gmg, 1)
    reduce_y(0)
    back_rows(0, gmg, 1)
    reduce_z(0)
    halos_add(0, 1)
    input_grad(1)
    stores = [load(ig_buf, ig_out)]
    spread_core(1)
    reduce_owner(0)
    adam(0)
    stores += [load(adam_out.at[k], ref) for k, ref in enumerate((master_out, moment_out, second_out))]
    spread_y(0)
    spread_wait(1)
    stores.append(load(slabs.at[1], slab_out.at[1]))
    spread_core(0)
    spread_wait(0)
    stores.append(load(slabs.at[0], slab_out.at[0]))
    for copy in stores:
        copy.wait()
    for copy, when in sends:
        if when is None:
            copy.wait_send()
        else:
            pl.when(when)(copy.wait_send)
    assert pool.used <= sems.shape[0], pool.used


def on_device(section_input, middle, out_grad, kernels, master, moment, second):
    any_space = pl.BlockSpec(memory_space=pl.ANY)
    flat = lambda a: a.reshape(2, PX, 128)
    owned = lambda a: a.reshape(2, 9, 8, 128)
    state = jax.ShapeDtypeStruct((2, 9, 8, 128), F32)
    outs = pl.pallas_call(
        kernel,
        out_shape=(
            jax.ShapeDtypeStruct((2, PX, 128), BF),
            jax.ShapeDtypeStruct((2, 4, 16, SLAB, 128), BF),
            state, state, state,
        ),
        in_specs=[any_space] * 7,
        out_specs=[any_space] * 5,
        scratch_shapes=[
            pltpu.VMEM((2, PX + 256, 128), BF),
            pltpu.VMEM((2, PX + 256, 128), BF),
            pltpu.VMEM((2, PX + 256, 512), BF),
            pltpu.VMEM((2, PX + 256, 512), BF),
            pltpu.VMEM((2, 9, 128, 512), BF),
            pltpu.VMEM((2, 384, PX + 256), BF),
            pltpu.VMEM((2, 4, 9, 128, 128), F32),
            pltpu.VMEM((PX, 128), F32),
            pltpu.VMEM((2, 2, 2, 128, 128), F32),
            pltpu.VMEM((2, 2, 2, 128, 128), F32),
            pltpu.VMEM((2, 2, 9, 128, 128), F32),
            pltpu.VMEM((2, 4, 2, 9, 32, 128), BF),
            pltpu.VMEM((2, 3, 2, 9, 32, 128), BF),
            pltpu.VMEM((2, 8, SLAB, 128), BF),
            pltpu.VMEM((2, 7, SLAB, 128), BF),
            pltpu.VMEM((2, 9, 8, 128), F32),
            pltpu.VMEM((2, 9, 8, 128), F32),
            pltpu.VMEM((3, 2, 9, 8, 128), F32),
            pltpu.VMEM((3, 2, 9, 8, 128), F32),
            pltpu.VMEM((2, 4, 16, SLAB, 128), BF),
            pltpu.VMEM((2, PX, 128), BF),
            pltpu.SemaphoreType.DMA((400,)),
        ],
        compiler_params=pltpu.CompilerParams(
            collective_id=0, has_side_effects=True, vmem_limit_bytes=VMEM_LIMIT
        ),
        cost_estimate=pl.CostEstimate(flops=10**10, bytes_accessed=10**7, transcendentals=10**6),
    )(
        flat(section_input), flat(middle), flat(out_grad),
        kernels.reshape(2, 9, 512, 128), owned(master), owned(moment), owned(second),
    )
    input_grad, slabs, new_master, new_moment, new_second = outs
    new_kernels = slabs[:, :, :, 0:72, :].reshape(2, 64, 9, 8, 128).transpose(0, 2, 1, 3, 4)
    back_shape = lambda a: a.reshape(master.shape)
    return (
        input_grad.reshape(section_input.shape),
        new_kernels.reshape(kernels.shape),
        back_shape(new_master), back_shape(new_moment), back_shape(new_second),
    )


def solution(mesh):
    activation = P("dp", None, "space", None, "chan")
    state = P(None, None, None, ("dp", "space"), "chan")
    weights = P(None, None, None, None, "chan")
    return jax.shard_map(
        on_device,
        mesh=mesh,
        in_specs=(activation, activation, activation, weights, state, state, state),
        out_specs=(activation, weights, state, state, state),
        check_vma=False,
    )
```

```python
import jax
import jax.numpy as jnp
from jax import lax
from jax.experimental import pallas as pl
from jax.experimental.pallas import tpu as pltpu
from jax.sharding import PartitionSpec as P

BF = jnp.bfloat16
F32 = jnp.float32
MESH = pl.DeviceIdType.MESH
PX = 1024
SLAB = 80
SEMS = 440
VMEM_LIMIT = 56 * 1024 * 1024


def sigmoid(v):
    return 1.0 / (1.0 + jnp.exp(-v))


def dsilu(v):
    sig = sigmoid(v)
    return sig * (1.0 + v * (1.0 - sig))


def nt_dot(a, b):
    return lax.dot_general(a, b, (((1,), (1,)), ((), ())), preferred_element_type=F32)


class Sems:
    def __init__(self, ref):
        self.ref = ref
        self.used = 0

    def take(self, count=1):
        base = self.used
        self.used += count
        return base


def kernel(
    x_in, mid_in, og_in, kern, master, moment, second,
    ig_out, kern_out, master_out, moment_out, second_out,
    xpad, midpad, gog, gmg, w, actt, red, back, halo_in, halo_out, core_in,
    ysend, yrecv, zsend, zrecv, adam_in, adam_out, slabs, new_kern, ig_buf, sems,
):
    chan = lax.axis_index("chan")
    dp = lax.axis_index("dp")
    space = lax.axis_index("space")
    z_hi, core = dp // 2, dp % 2
    z_lo, y = space // 4, space % 4
    z = z_hi * 4 + z_lo
    pool = Sems(sems)
    sends = []

    def at_chan(p):
        return {"chan": (chan + p) % 4}

    def at_y(p):
        return {"space": z_lo * 4 + (y + p) % 4}

    def at_z(p):
        other = (z + p) % 8
        return {"dp": (other // 4) * 2 + core, "space": (other % 4) * 4 + y}

    sibling = {"dp": z_hi * 2 + (1 - core)}
    has_prev = space > 0
    has_next = space < 15
    on_diagonal = chan == dp

    def send(src, dst, target, recv_sem, when=None):
        copy = pltpu.make_async_remote_copy(
            src_ref=src, dst_ref=dst, send_sem=sems.at[pool.take()], recv_sem=sems.at[recv_sem],
            device_id=target, device_id_type=MESH,
        )
        if when is None:
            copy.start()
        else:
            pl.when(when)(copy.start)
        sends.append((copy, when))

    def wait_in(dst, sem):
        pltpu.make_async_copy(dst, dst, sems.at[sem]).wait()

    def load(src, dst):
        copy = pltpu.make_async_copy(src, dst, sems.at[pool.take()])
        copy.start()
        return copy

    inside = pl.ds(128, PX)
    load_mid = load(mid_in, midpad.at[:, inside, :])
    load_x = load(x_in, xpad.at[:, inside, :])
    load_og = load(og_in, gog.at[:, inside, pl.ds(0, 128)])
    my_rows = pl.ds(core * 64 + y * 16, 16)
    load_w = [
        load(kern.at[l, :, pl.ds(chan * 128 + core * 64 + y * 16, 16), :], w.at[l, :, my_rows, pl.ds(0, 128)])
        for l in range(2)
    ]
    load_adam = [load(ref, adam_in.at[k]) for k, ref in enumerate((master, moment, second))]

    barrier = pltpu.get_barrier_semaphore()

    def greet(target):
        pl.semaphore_signal(barrier, inc=1, device_id=target, device_id_type=MESH)

    for p in range(1, 4):
        greet(at_chan(p))
        greet(at_y(p))
    for p in range(1, 8):
        greet(at_z(p))
    greet(sibling)
    prev, nxt = {"space": space - 1}, {"space": space + 1}
    pl.when(has_prev)(lambda: greet(prev))
    pl.when(has_next)(lambda: greet(nxt))
    for q in range(8):
        source = {"dp": (q // 4) * 2 + chan % 2, "chan": dp, "space": (q % 4) * 4 + y}
        pl.when(jnp.logical_not(on_diagonal & (z == q)))(lambda source=source: greet(source))

    zero_row = jnp.zeros((128, 512), BF)
    for g in (gog, gmg):
        for f in range(2):
            g[f, pl.ds(0, 128), :] = zero_row
            g[f, pl.ds(128 + PX, 128), :] = zero_row

    @pl.when(space == 0)
    def _():
        for pad in (midpad, xpad):
            pad[:, pl.ds(0, 128), :] = jnp.zeros((2, 128, 128), BF)

    @pl.when(space == 15)
    def _():
        for pad in (midpad, xpad):
            pad[:, pl.ds(128 + PX, 128), :] = jnp.zeros((2, 128, 128), BF)

    expected = 22 + has_prev.astype(jnp.int32) + has_next.astype(jnp.int32) - on_diagonal.astype(jnp.int32)
    pl.semaphore_wait(barrier, expected)

    gathers = {}

    def half(f, h):
        return (f, pl.ds(128 + 512 * h, 512))

    def gather_own(name, g, src, f):
        sem = gathers.setdefault(name, {})
        for k in ("left", "right", "far"):
            for h in range(2):
                sem[k, f, h] = pool.take()
        for step in range(2):
            h = step
            send(src(f, h), g.at[(*half(f, h), pl.ds(128, 128))], at_chan(1), sem["left", f, h])
            h = 1 - step
            send(src(f, h), g.at[(*half(f, h), pl.ds(384, 128))], at_chan(3), sem["right", f, h])

    def gather_forward(name, g, f):
        sem = gathers[name]
        here = g.at[(*half(f, 0), pl.ds(128, 128))]
        wait_in(here, sem["left", f, 0])
        send(here, g.at[(*half(f, 0), pl.ds(256, 128))], at_chan(1), sem["far", f, 0])
        here = g.at[(*half(f, 1), pl.ds(384, 128))]
        wait_in(here, sem["right", f, 1])
        send(here, g.at[(*half(f, 1), pl.ds(256, 128))], at_chan(3), sem["far", f, 1])

    def gather_wait(name, g, f):
        sem = gathers[name]
        wait_in(g.at[(*half(f, 1), pl.ds(128, 128))], sem["left", f, 1])
        wait_in(g.at[(*half(f, 0), pl.ds(384, 128))], sem["right", f, 0])
        for h in range(2):
            wait_in(g.at[(*half(f, h), pl.ds(256, 128))], sem["far", f, h])

    w_sem = {}

    def weights_chan(l):
        for p in range(1, 4):
            w_sem["x", l, p] = pool.take()
            their = (chan + p) % 4
            send(
                kern.at[l, :, pl.ds(their * 128 + core * 64 + y * 16, 16), :],
                w.at[l, :, my_rows, pl.ds(128 * p, 128)],
                at_chan(p), w_sem["x", l, p],
            )

    def weights_y(l):
        load_w[l].wait()
        for p in range(1, 4):
            wait_in(w.at[l, :, my_rows, pl.ds(128 * p, 128)], w_sem["x", l, p])
        for p in range(1, 4):
            w_sem["y", l, p] = pool.take()
            here = w.at[l, :, my_rows, :]
            send(here, here, at_y(p), w_sem["y", l, p])

    def weights_core(l):
        for p in range(4):
            if p:
                wait_in(w.at[l, :, pl.ds(core * 64 + ((y + 4 - p) % 4) * 16, 16), :], w_sem["y", l, p])
            w_sem["core", l, p] = pool.take()
            here = w.at[l, :, pl.ds(core * 64 + ((y + 4 - p) % 4) * 16, 16), :]
            send(here, here, sibling, w_sem["core", l, p])

    def weights_wait(l):
        for p in range(4):
            wait_in(w.at[l, :, pl.ds((1 - core) * 64 + ((y + 4 - p) % 4) * 16, 16), :], w_sem["core", l, p])

    rim_sem = {}

    def rims(k, src, pad):
        up, down = pool.take(), pool.take()
        rim_sem[k] = (up, down)
        send(src.at[:, pl.ds(PX - 128, 128), :], pad.at[:, pl.ds(0, 128), :], nxt, up, has_next)
        send(src.at[:, pl.ds(0, 128), :], pad.at[:, pl.ds(128 + PX, 128), :], prev, down, has_prev)

    def rims_wait(k, pad):
        up, down = rim_sem[k]
        pl.when(has_prev)(lambda: wait_in(pad.at[:, pl.ds(0, 128), :], up))
        pl.when(has_next)(lambda: wait_in(pad.at[:, pl.ds(128 + PX, 128), :], down))

    def transpose_act(pad):
        lane = lax.broadcasted_iota(jnp.int32, (128, 128), 1)

        def body(i, carry):
            f, row = i // 10, i % 10
            v = pad[f, pl.ds(row * 128, 128), :].astype(F32)
            a = (v * sigmoid(v)).astype(BF).astype(F32).T
            at = pl.ds(pl.multiple_of(row * 128, 128), 128)
            before = jnp.where(lane == 0, 0.0, pltpu.roll(a, 1, 1))
            after = jnp.where(lane == 127, 0.0, pltpu.roll(a, 127, 1))
            actt[f, pl.ds(0, 128), at] = before.astype(BF)
            actt[f, pl.ds(128, 128), at] = a.astype(BF)
            actt[f, pl.ds(256, 128), at] = after.astype(BF)
            return carry

        lax.fori_loop(0, 20, body, 0)

    def kernel_grad(l, g, f):
        cotangent = g[f, inside, :]
        for r in range(3):
            part = jnp.dot(actt[f, :, pl.ds(128 * r, PX)], cotangent, preferred_element_type=F32)
            for k in range(4):
                block = part[:, 128 * k : 128 * k + 128].reshape(3, 128, 128)
                if f:
                    block = block + red[l, k, pl.ds(3 * r, 3)]
                red[l, k, pl.ds(3 * r, 3)] = block

    def weight_rows(l, r):
        return w[l, pl.ds(3 * r, 3)].reshape(384, 512)

    def join_taps(acc):
        rows = acc.shape[0]
        col = lax.broadcasted_iota(jnp.int32, (rows, 128), 0) % 128
        first = jnp.where(col == 127, 0.0, pltpu.roll(acc[:, 0:128], rows - 1, 0))
        last = jnp.where(col == 0, 0.0, pltpu.roll(acc[:, 256:384], 1, 0))
        return first + acc[:, 128:256] + last

    halo_sem = {}

    def back_halos(l, g, f):
        up, down = pool.take(), pool.take()
        halo_sem[l, f] = (up, down)
        halo_out[l, f, 0] = join_taps(nt_dot(g[f, pl.ds(128, 128), :], weight_rows(l, 0)))
        halo_out[l, f, 1] = join_taps(nt_dot(g[f, pl.ds(PX, 128), :], weight_rows(l, 2)))
        send(halo_out.at[l, f, 0], halo_in.at[l, f, 1], prev, down, has_prev)
        send(halo_out.at[l, f, 1], halo_in.at[l, f, 0], nxt, up, has_next)

    def back_rows(l, g, f):
        def body(i, carry):
            start = i * 256
            acc = jnp.zeros((256, 384), F32)
            for r in range(3):
                rows = pl.ds(pl.multiple_of(start + (2 - r) * 128, 128), 256)
                acc = acc + nt_dot(g[f, rows, :], weight_rows(l, r))
            back[pl.ds(pl.multiple_of(start, 128), 256), :] = join_taps(acc)
            return carry

        lax.fori_loop(0, 4, body, 0)

    def halos_add(l, f):
        up, down = halo_sem[l, f]

        @pl.when(has_prev)
        def _():
            wait_in(halo_in.at[l, f, 0], up)
            back[pl.ds(0, 128), :] = back[pl.ds(0, 128), :] + halo_in[l, f, 0]

        @pl.when(has_next)
        def _():
            wait_in(halo_in.at[l, f, 1], down)
            back[pl.ds(PX - 128, 128), :] = back[pl.ds(PX - 128, 128), :] + halo_in[l, f, 1]

    def middle_grad(f):
        def body(i, carry):
            rows = pl.ds(pl.multiple_of(i * 128, 128), 128)
            padded = pl.ds(pl.multiple_of(i * 128 + 128, 128), 128)
            v = midpad[f, padded, :].astype(F32)
            gmg[f, padded, pl.ds(0, 128)] = (back[rows, :] * dsilu(v)).astype(BF)
            return carry

        lax.fori_loop(0, 8, body, 0)

    def input_grad(f):
        def body(i, carry):
            rows = pl.ds(pl.multiple_of(i * 128, 128), 128)
            padded = pl.ds(pl.multiple_of(i * 128 + 128, 128), 128)
            v = xpad[f, padded, :].astype(F32)
            og = gog[f, padded, pl.ds(0, 128)].astype(F32)
            ig_buf[f, rows, :] = (og + back[rows, :] * dsilu(v)).astype(BF)
            return carry

        lax.fori_loop(0, 8, body, 0)

    r_sem = {}

    def slot_of(block):
        return (chan + 4 - block) % 4

    def reduce_core(l):
        for h in range(2):
            r_sem["core", l, h] = pool.take()
            send(red.at[l, slot_of(2 * h + 1 - core)], core_in.at[l, h], sibling, r_sem["core", l, h])

    def as_slab(v):
        return jnp.concatenate([v.reshape(72, 128), jnp.zeros((8, 128), F32)], axis=0).astype(BF)

    near_last = (2, 3, 1, 0)

    def reduce_y(l):
        for h in range(2):
            wait_in(core_in.at[l, h], r_sem["core", l, h])
        for p in (2, 1, 3, 0):
            q = (y + p) % 4

            def body(c, carry, q=q):
                rows = pl.ds(pl.multiple_of(c * 32 + q * 8, 8), 8)
                for h in range(2):
                    total = red[l, slot_of(2 * h + core), :, rows, :] + core_in[l, h, :, rows, :]
                    ysend[l, q, c, h] = as_slab(total)
                return carry

            lax.fori_loop(0, 4, body, 0)
            if p:
                for j in near_last:
                    r_sem["y", l, p, j] = pool.take()
                    send(ysend.at[l, q, (z_lo + j) % 4], yrecv.at[l, p - 1, j], at_y(p), r_sem["y", l, p, j])

    def reduce_z(l):
        r_sem["z", l] = pool.take(8)
        for j in near_last:
            c = (z_lo + j) % 4
            for p in range(1, 4):
                wait_in(yrecv.at[l, p - 1, j], r_sem["y", l, p, j])
            for h in range(2):
                total = ysend[l, y, c, h].astype(F32)
                for p in range(3):
                    total = total + yrecv[l, p, j, h].astype(F32)
                total = total.astype(BF)
                zsend[l, j, h] = total
                owner = {"chan": 2 * h + core, "dp": chan, "space": c * 4 + y}
                mine = on_diagonal & (z_hi == h)
                away = jnp.logical_not(mine) if j == 0 else None
                send(zsend.at[l, j, h], zrecv.at[l, z], owner, r_sem["z", l] + z, away)
                if j == 0:

                    @pl.when(mine)
                    def _(total=total):
                        zrecv[l, z] = total

    a_sem = {}
    by_distance = (0, 1, 7, 2, 6, 3, 5, 4)

    def z_from(d):
        other = (z + 8 - d) % 8
        return (other // 4) * 2 + core, other % 4

    def adam(l):
        if l == 1:
            for copy in load_adam:
                copy.wait()
        for q in range(8):
            there = jnp.logical_not(on_diagonal & (z == q))
            pl.when(there)(lambda q=q: wait_in(zrecv.at[l, q], r_sem["z", l] + q))
        grads = zrecv[l, 0].astype(F32)
        for q in range(1, 8):
            grads = grads + zrecv[l, q].astype(F32)
        grads = grads[0:72].reshape(9, 8, 128)
        new_moment = 0.9 * adam_in[1, l] + 0.1 * grads
        new_second = 0.999 * adam_in[2, l] + 0.001 * grads * grads
        corrected = new_moment / (1.0 - 0.9**10)
        scale_term = jnp.sqrt(new_second / (1.0 - 0.999**10)) + 1e-08
        new_master = adam_in[0, l] - 0.01 * corrected / scale_term
        slabs[l, dp, space] = as_slab(new_master)
        here = slabs.at[l, dp, space]
        for p in by_distance[1:]:
            a_sem["z", l, p] = pool.take()
            send(here, here, at_z(p), a_sem["z", l, p])
        to_y(l, 0)
        adam_out[0, l] = new_master
        adam_out[1, l] = new_moment
        adam_out[2, l] = new_second

    def to_y(l, d):
        dp_there, z_there = z_from(d)
        here = slabs.at[l, dp_there, z_there * 4 + y]
        for p in range(1, 4):
            a_sem["y", l, p, d] = pool.take()
            send(here, here, at_y(p), a_sem["y", l, p, d])

    def spread_y(l):
        for d in by_distance[1:]:
            dp_there, z_there = z_from(d)
            wait_in(slabs.at[l, dp_there, z_there * 4 + y], a_sem["z", l, d])
            to_y(l, d)

    def assemble(l, dp_there, z_there):
        for pair in range(2):
            both = [
                slabs[l, dp_there, z_there * 4 + 2 * pair + i].astype(F32)[0:72].reshape(9, 8, 128) for i in range(2)
            ]
            rows = pl.ds(pl.multiple_of(dp_there * 128 + z_there * 32 + pair * 16, 16), 16)
            new_kern[l, :, rows, :] = jnp.concatenate(both, axis=1).astype(BF)

    def spread_core(l):
        for d in by_distance:
            dp_there, z_there = z_from(d)
            for p in range(1, 4):
                wait_in(slabs.at[l, dp_there, z_there * 4 + (y + 4 - p) % 4], a_sem["y", l, p, d])
            a_sem["core", l, d] = pool.take()
            here = slabs.at[l, dp_there, pl.ds(z_there * 4, 4)]
            send(here, here, sibling, a_sem["core", l, d])
            assemble(l, dp_there, z_there)

    def spread_wait(l):
        for d in by_distance:
            dp_there, z_there = z_from(d)
            dp_there = dp_there + 1 - 2 * core
            wait_in(slabs.at[l, dp_there, pl.ds(z_there * 4, 4)], a_sem["core", l, d])
            assemble(l, dp_there, z_there)

    def og_half(f, h):
        return og_in.at[f, pl.ds(512 * h, 512), :]

    def mg_half(f, h):
        return gmg.at[(*half(f, h), pl.ds(0, 128))]

    weights_chan(1)
    gather_own("og", gog, og_half, 0)
    rims("mid", mid_in, midpad)
    weights_y(1)
    gather_forward("og", gog, 0)
    weights_chan(0)
    gather_own("og", gog, og_half, 1)
    load_mid.wait()
    rims_wait("mid", midpad)
    transpose_act(midpad)
    gather_wait("og", gog, 0)
    load_og.wait()
    kernel_grad(1, gog, 0)
    gather_forward("og", gog, 1)
    weights_core(1)
    rims("x", x_in, xpad)
    weights_y(0)
    weights_wait(1)
    back_halos(1, gog, 0)
    back_rows(1, gog, 0)
    halos_add(1, 0)
    middle_grad(0)
    gather_own("mg", gmg, mg_half, 0)
    gather_wait("og", gog, 1)
    back_halos(1, gog, 1)
    kernel_grad(1, gog, 1)
    reduce_core(1)
    back_rows(1, gog, 1)
    gather_forward("mg", gmg, 0)
    halos_add(1, 1)
    middle_grad(1)
    gather_own("mg", gmg, mg_half, 1)
    reduce_y(1)
    weights_core(0)
    load_x.wait()
    rims_wait("x", xpad)
    transpose_act(xpad)
    weights_wait(0)
    gather_wait("mg", gmg, 0)
    kernel_grad(0, gmg, 0)
    gather_forward("mg", gmg, 1)
    back_halos(0, gmg, 0)
    back_rows(0, gmg, 0)
    reduce_z(1)
    halos_add(0, 0)
    input_grad(0)
    gather_wait("mg", gmg, 1)
    kernel_grad(0, gmg, 1)
    reduce_core(0)
    back_halos(0, gmg, 1)
    reduce_y(0)
    adam(1)
    back_rows(0, gmg, 1)
    halos_add(0, 1)
    input_grad(1)
    stores = [load(ig_buf, ig_out)]
    reduce_z(0)
    spread_y(1)
    adam(0)
    stores += [load(adam_out.at[k], ref) for k, ref in enumerate((master_out, moment_out, second_out))]
    spread_core(1)
    spread_y(0)
    spread_wait(1)
    stores.append(load(new_kern.at[1], kern_out.at[1]))
    spread_core(0)
    spread_wait(0)
    stores.append(load(new_kern.at[0], kern_out.at[0]))
    for copy in stores:
        copy.wait()
    for copy, when in sends:
        if when is None:
            copy.wait_send()
        else:
            pl.when(when)(copy.wait_send)
    assert pool.used <= sems.shape[0], pool.used


def hand_over(ig, kern, master, moment, second, *refs):
    outs, held, sems = refs[:5], refs[5:10], refs[10]
    parts = [(1, (l, pl.ds(3 * r, 3))) for l in range(2) for r in range(3)]
    parts += [(0, (f,)) for f in range(2)] + [(k, (l,)) for k in (2, 3, 4) for l in range(2)]
    ins = (ig, kern, master, moment, second)
    steps = []
    for i, (k, at) in enumerate(parts):
        arrive = pltpu.make_async_copy(ins[k].at[at], held[k].at[at], sems.at[0, i])
        leave = pltpu.make_async_copy(held[k].at[at], outs[k].at[at], sems.at[1, i])
        arrive.start()
        steps.append((arrive, leave))
    for arrive, leave in steps:
        arrive.wait()
        leave.start()
    for arrive, leave in steps:
        leave.wait()


def on_device(section_input, middle, out_grad, kernels, master, moment, second):
    any_space = pl.BlockSpec(memory_space=pl.ANY)
    flat = lambda a: a.reshape(2, PX, 128)
    owned = lambda a: a.reshape(2, 9, 8, 128)
    state = jax.ShapeDtypeStruct((2, 9, 8, 128), F32)
    results = (
        jax.ShapeDtypeStruct((2, PX, 128), BF),
        jax.ShapeDtypeStruct((2, 9, 512, 128), BF),
        state, state, state,
    )
    outs = pl.pallas_call(
        kernel,
        out_shape=results,
        in_specs=[any_space] * 7,
        out_specs=[any_space] * 5,
        scratch_shapes=[
            pltpu.VMEM((2, PX + 256, 128), BF),
            pltpu.VMEM((2, PX + 256, 128), BF),
            pltpu.VMEM((2, PX + 256, 512), BF),
            pltpu.VMEM((2, PX + 256, 512), BF),
            pltpu.VMEM((2, 9, 128, 512), BF),
            pltpu.VMEM((2, 384, PX + 256), BF),
            pltpu.VMEM((2, 4, 9, 128, 128), F32),
            pltpu.VMEM((PX, 128), F32),
            pltpu.VMEM((2, 2, 2, 128, 128), F32),
            pltpu.VMEM((2, 2, 2, 128, 128), F32),
            pltpu.VMEM((2, 2, 9, 128, 128), F32),
            pltpu.VMEM((2, 4, 4, 2, SLAB, 128), BF),
            pltpu.VMEM((2, 3, 4, 2, SLAB, 128), BF),
            pltpu.VMEM((2, 4, 2, SLAB, 128), BF),
            pltpu.VMEM((2, 8, SLAB, 128), BF),
            pltpu.VMEM((3, 2, 9, 8, 128), F32),
            pltpu.VMEM((3, 2, 9, 8, 128), F32),
            pltpu.VMEM((2, 4, 16, SLAB, 128), BF),
            pltpu.VMEM((2, 9, 512, 128), BF),
            pltpu.VMEM((2, PX, 128), BF),
            pltpu.SemaphoreType.DMA((SEMS,)),
        ],
        compiler_params=pltpu.CompilerParams(
            collective_id=0, has_side_effects=True, vmem_limit_bytes=VMEM_LIMIT
        ),
        cost_estimate=pl.CostEstimate(flops=10**10, bytes_accessed=10**7, transcendentals=10**6),
    )(
        flat(section_input), flat(middle), flat(out_grad),
        kernels.reshape(2, 9, 512, 128), owned(master), owned(moment), owned(second),
    )
    outs = pl.pallas_call(
        hand_over,
        out_shape=results,
        in_specs=[any_space] * 5,
        out_specs=[any_space] * 5,
        scratch_shapes=[pltpu.VMEM(r.shape, r.dtype) for r in results] + [pltpu.SemaphoreType.DMA((2, 14))],
    )(*outs)
    shapes = (section_input.shape, kernels.shape, master.shape, master.shape, master.shape)
    return tuple(out.reshape(shape) for out, shape in zip(outs, shapes))


def solution(mesh):
    activation = P("dp", None, "space", None, "chan")
    state = P(None, None, None, ("dp", "space"), "chan")
    weights = P(None, None, None, None, "chan")
    return jax.shard_map(
        on_device,
        mesh=mesh,
        in_specs=(activation, activation, activation, weights, state, state, state),
        out_specs=(activation, weights, state, state, state),
        check_vma=False,
    )
```

```python
import jax
import jax.numpy as jnp
from jax import lax
from jax.experimental import pallas as pl
from jax.experimental.pallas import tpu as pltpu
from jax.sharding import PartitionSpec as P

BF = jnp.bfloat16
F32 = jnp.float32
MESH = pl.DeviceIdType.MESH
PX = 1024
SLAB = 80
SEMS = 520
VMEM_LIMIT = 56 * 1024 * 1024


def sigmoid(v):
    return 1.0 / (1.0 + jnp.exp(-v))


def dsilu(v):
    sig = sigmoid(v)
    return sig * (1.0 + v * (1.0 - sig))


def nt_dot(a, b):
    return lax.dot_general(a, b, (((1,), (1,)), ((), ())), preferred_element_type=F32)


class Sems:
    def __init__(self, ref):
        self.ref = ref
        self.used = 0

    def take(self, count=1):
        base = self.used
        self.used += count
        return base


def kernel(
    x_in, mid_in, og_in, kern, master, moment, second,
    ig_out, kern_out, master_out, moment_out, second_out,
    xpad, midpad, gog, gmg, w, actt, red, back, halo_in, halo_out, core_in,
    ysend, yrecv, zsend, zrecv, adam_in, adam_out, slabs, new_kern, ig_buf, sems, meet,
):
    chan = lax.axis_index("chan")
    dp = lax.axis_index("dp")
    space = lax.axis_index("space")
    z_hi, core = dp // 2, dp % 2
    z_lo, y = space // 4, space % 4
    z = z_hi * 4 + z_lo
    pool = Sems(sems)
    sends = []

    def at_chan(p):
        return {"chan": (chan + p) % 4}

    def at_y(p):
        return {"space": z_lo * 4 + (y + p) % 4}

    def at_z_lo(p):
        return {"space": ((z_lo + p) % 4) * 4 + y}

    def at_z(p):
        other = (z + p) % 8
        return {"dp": (other // 4) * 2 + core, "space": (other % 4) * 4 + y}

    sibling = {"dp": z_hi * 2 + (1 - core)}
    has_prev = space > 0
    has_next = space < 15
    on_diagonal = chan == dp

    def send(src, dst, target, recv_sem, when=None):
        copy = pltpu.make_async_remote_copy(
            src_ref=src, dst_ref=dst, send_sem=sems.at[pool.take()], recv_sem=sems.at[recv_sem],
            device_id=target, device_id_type=MESH,
        )
        if when is None:
            copy.start()
        else:
            pl.when(when)(copy.start)
        sends.append((copy, when))

    def wait_in(dst, sem):
        pltpu.make_async_copy(dst, dst, sems.at[sem]).wait()

    def load(src, dst):
        copy = pltpu.make_async_copy(src, dst, sems.at[pool.take()])
        copy.start()
        return copy

    barrier = pltpu.get_barrier_semaphore()

    def signal(sem, target):
        pl.semaphore_signal(sem, inc=1, device_id=target, device_id_type=MESH)

    prev, nxt = {"space": space - 1}, {"space": space + 1}
    first_z, last_z = z_lo == 0, z_lo == 3
    for p in range(1, 4):
        signal(barrier, at_chan(p))
        signal(barrier, at_y(p))
        signal(barrier, at_z_lo(p))
    signal(barrier, sibling)
    pl.when(has_prev)(lambda: signal(barrier, prev))
    pl.when(has_next)(lambda: signal(barrier, nxt))
    pl.when(first_z)(lambda: signal(barrier, at_z(7)))

    inside = pl.ds(128, PX)
    load_mid = load(mid_in, midpad.at[:, inside, :])
    load_x = load(x_in, xpad.at[:, inside, :])
    load_og = load(og_in, gog.at[:, inside, pl.ds(0, 128)])
    w_parts = ((pl.ds(0, 6), y, at_y), (pl.ds(6, 3), z_lo, at_z_lo))

    def w_rows(index, core=core):
        return pl.ds(core * 64 + index * 16, 16)

    load_w = {
        (l, i): load(
            kern.at[l, taps, pl.ds(chan * 128 + core * 64 + index * 16, 16), :], w.at[l, taps, w_rows(index), pl.ds(0, 128)]
        )
        for l in (1, 0)
        for i, (taps, index, _) in enumerate(w_parts)
    }
    load_adam = [load(ref, adam_in.at[k]) for k, ref in enumerate((master, moment, second))]


    expected = 10 + has_prev.astype(jnp.int32) + has_next.astype(jnp.int32) + last_z.astype(jnp.int32)
    pl.semaphore_wait(barrier, expected)

    def hear_half():
        pl.when(last_z)(lambda: signal(meet.at[0], at_z(1)))

    def hear_ring():
        @pl.when(first_z)
        def _():
            pl.semaphore_wait(meet.at[0], 1)
            for p in range(1, 4):
                signal(meet.at[1], at_z_lo(p))

    def hear_sibling():
        pl.when(jnp.logical_not(first_z))(lambda: pl.semaphore_wait(meet.at[1], 1))
        signal(meet.at[2], sibling)

    def hear_chan():
        pl.semaphore_wait(meet.at[2], 1)
        for p in range(1, 4):
            signal(meet.at[3], at_chan(p))

    def hear_all():
        pl.semaphore_wait(meet.at[3], 3)

    def clear_edges():
        zero_row = jnp.zeros((128, 512), BF)
        for g in (gog, gmg):
            for f in range(2):
                g[f, pl.ds(0, 128), :] = zero_row
                g[f, pl.ds(128 + PX, 128), :] = zero_row

        @pl.when(space == 0)
        def _():
            for pad in (midpad, xpad):
                pad[:, pl.ds(0, 128), :] = jnp.zeros((2, 128, 128), BF)

        @pl.when(space == 15)
        def _():
            for pad in (midpad, xpad):
                pad[:, pl.ds(128 + PX, 128), :] = jnp.zeros((2, 128, 128), BF)

    gathers = {}

    pieces = range(4)

    def piece(f, i):
        return (f, pl.ds(128 + 256 * i, 256))

    def gather_own(name, g, src, f, order):
        sem = gathers.setdefault(name, {})
        for i in order:
            for k in ("left", "right", "far"):
                sem[k, f, i] = pool.take()
        for i, j in zip(order, tuple(order)[::-1]):
            send(src(f, i), g.at[(*piece(f, i), pl.ds(128, 128))], at_chan(1), sem["left", f, i])
            send(src(f, j), g.at[(*piece(f, j), pl.ds(384, 128))], at_chan(3), sem["right", f, j])

    def gather_forward(name, g, f, order):
        sem = gathers[name]
        for i in order:
            k, lanes, target = ("left", 128, at_chan(1)) if i < 2 else ("right", 384, at_chan(3))
            here = g.at[(*piece(f, i), pl.ds(lanes, 128))]
            wait_in(here, sem[k, f, i])
            send(here, g.at[(*piece(f, i), pl.ds(256, 128))], target, sem["far", f, i])

    def gather_wait(name, g, f):
        sem = gathers[name]
        for i in pieces:
            k, lanes = ("right", 384) if i < 2 else ("left", 128)
            wait_in(g.at[(*piece(f, i), pl.ds(lanes, 128))], sem[k, f, i])
            wait_in(g.at[(*piece(f, i), pl.ds(256, 128))], sem["far", f, i])

    w_sem = {}

    def weights_chan(l):
        for i, (taps, index, _) in enumerate(w_parts):
            for p in range(1, 4):
                w_sem["x", l, i, p] = pool.take()
                their = (chan + p) % 4
                send(
                    kern.at[l, taps, pl.ds(their * 128 + core * 64 + index * 16, 16), :],
                    w.at[l, taps, w_rows(index), pl.ds(128 * p, 128)],
                    at_chan(p), w_sem["x", l, i, p],
                )

    def weights_group(l):
        for i, (taps, index, at_peer) in enumerate(w_parts):
            load_w[l, i].wait()
            for p in range(1, 4):
                wait_in(w.at[l, taps, w_rows(index), pl.ds(128 * p, 128)], w_sem["x", l, i, p])
            here = w.at[l, taps, w_rows(index), :]
            for p in (2, 1, 3):
                w_sem["group", l, i, p] = pool.take()
                send(here, here, at_peer(p), w_sem["group", l, i, p])

    def weights_core(l):
        for p in (0, 1, 3, 2):
            for i, (taps, index, _) in enumerate(w_parts):
                here = w.at[l, taps, w_rows((index + 4 - p) % 4), :]
                if p:
                    wait_in(here, w_sem["group", l, i, p])
                w_sem["core", l, i, p] = pool.take()
                send(here, here, sibling, w_sem["core", l, i, p])

    def weights_wait(l):
        for p in (0, 1, 3, 2):
            for i, (taps, index, _) in enumerate(w_parts):
                wait_in(w.at[l, taps, w_rows((index + 4 - p) % 4, 1 - core), :], w_sem["core", l, i, p])

    rim_sem = {}

    def rims(k, src, pad):
        up, down = pool.take(), pool.take()
        rim_sem[k] = (up, down)
        send(src.at[:, pl.ds(PX - 128, 128), :], pad.at[:, pl.ds(0, 128), :], nxt, up, has_next)
        send(src.at[:, pl.ds(0, 128), :], pad.at[:, pl.ds(128 + PX, 128), :], prev, down, has_prev)

    def rims_wait(k, pad):
        up, down = rim_sem[k]
        pl.when(has_prev)(lambda: wait_in(pad.at[:, pl.ds(0, 128), :], up))
        pl.when(has_next)(lambda: wait_in(pad.at[:, pl.ds(128 + PX, 128), :], down))

    def transpose_act(l, pad, first, step, count):
        lane = lax.broadcasted_iota(jnp.int32, (128, 128), 1)

        def body(i, carry):
            f, row = i // count, first + step * (i % count)
            v = pad[f, pl.ds(pl.multiple_of(row * 128, 128), 128), :].astype(F32)
            a = (v * sigmoid(v)).astype(BF).astype(F32).T
            at = pl.ds(pl.multiple_of(row * 128, 128), 128)
            before = jnp.where(lane == 0, 0.0, pltpu.roll(a, 1, 1))
            after = jnp.where(lane == 127, 0.0, pltpu.roll(a, 127, 1))
            actt[l, f, pl.ds(0, 128), at] = before.astype(BF)
            actt[l, f, pl.ds(128, 128), at] = a.astype(BF)
            actt[l, f, pl.ds(256, 128), at] = after.astype(BF)
            return carry

        lax.fori_loop(0, 2 * count, body, 0)

    def act_inner(l, pad):
        transpose_act(l, pad, 1, 1, 8)

    def act_rims(l, pad):
        transpose_act(l, pad, 0, 9, 2)

    def kernel_grad(l, g, f):
        cotangent = g[f, inside, :]
        for r in range(3):
            part = jnp.dot(actt[l, f, :, pl.ds(128 * r, PX)], cotangent, preferred_element_type=F32)
            for k in range(4):
                block = part[:, 128 * k : 128 * k + 128].reshape(3, 128, 128)
                if f:
                    block = block + red[l, k, pl.ds(3 * r, 3)]
                red[l, k, pl.ds(3 * r, 3)] = block
            if f:
                reduce_core(l, r)

    def weight_rows(l, r):
        return w[l, pl.ds(3 * r, 3)].reshape(384, 512)

    def join_taps(acc):
        rows = acc.shape[0]
        col = lax.broadcasted_iota(jnp.int32, (rows, 128), 0) % 128
        first = jnp.where(col == 127, 0.0, pltpu.roll(acc[:, 0:128], rows - 1, 0))
        last = jnp.where(col == 0, 0.0, pltpu.roll(acc[:, 256:384], 1, 0))
        return first + acc[:, 128:256] + last

    halo_sem = {}

    def back_halos(l, g, f):
        up, down = pool.take(), pool.take()
        halo_sem[l, f] = (up, down)
        halo_out[l, f, 0] = join_taps(nt_dot(g[f, pl.ds(128, 128), :], weight_rows(l, 0)))
        halo_out[l, f, 1] = join_taps(nt_dot(g[f, pl.ds(PX, 128), :], weight_rows(l, 2)))
        send(halo_out.at[l, f, 0], halo_in.at[l, f, 1], prev, down, has_prev)
        send(halo_out.at[l, f, 1], halo_in.at[l, f, 0], nxt, up, has_next)

    def back_rows(l, g, f, i):
        start = i * 256
        acc = jnp.zeros((256, 384), F32)
        for r in range(3):
            rows = pl.ds(pl.multiple_of(start + (2 - r) * 128, 128), 256)
            acc = acc + nt_dot(g[f, rows, :], weight_rows(l, r))
        return join_taps(acc)

    def back_inner(l, g, f):
        def body(i, carry):
            finish(l, f, i * 256, back_rows(l, g, f, i))
            return carry

        lax.fori_loop(1, 3, body, 0)

    def back_outer(l, g, f):
        def body(i, carry):
            back[pl.ds(pl.multiple_of(i * 256, 256), 256), :] = back_rows(l, g, f, i * 3)
            return carry

        lax.fori_loop(0, 2, body, 0)
        up, down = halo_sem[l, f]

        @pl.when(has_prev)
        def _():
            wait_in(halo_in.at[l, f, 0], up)
            back[pl.ds(0, 128), :] = back[pl.ds(0, 128), :] + halo_in[l, f, 0]

        @pl.when(has_next)
        def _():
            wait_in(halo_in.at[l, f, 1], down)
            back[pl.ds(384, 128), :] = back[pl.ds(384, 128), :] + halo_in[l, f, 1]

        def close(i, carry):
            finish(l, f, i * 768, back[pl.ds(pl.multiple_of(i * 256, 256), 256), :])
            return carry

        lax.fori_loop(0, 2, close, 0)

    def finish(l, f, start, total):
        rows = pl.ds(pl.multiple_of(start, 128), 256)
        padded = pl.ds(pl.multiple_of(start + 128, 128), 256)
        if l:
            v = midpad[f, padded, :].astype(F32)
            gmg[f, padded, pl.ds(0, 128)] = (total * dsilu(v)).astype(BF)
        else:
            v = xpad[f, padded, :].astype(F32)
            og = gog[f, padded, pl.ds(0, 128)].astype(F32)
            ig_buf[f, rows, :] = (og + total * dsilu(v)).astype(BF)

    r_sem = {}

    def slot_of(block):
        return (chan + 4 - block) % 4

    def reduce_core(l, r):
        for h in range(2):
            r_sem["core", l, h, r] = pool.take()
            taps = pl.ds(3 * r, 3)
            send(red.at[l, slot_of(2 * h + 1 - core), taps], core_in.at[l, h, taps], sibling, r_sem["core", l, h, r])

    def as_slab(v):
        return jnp.concatenate([v.reshape(72, 128), jnp.zeros((8, 128), F32)], axis=0).astype(BF)

    near_last = (2, 3, 1, 0)

    def reduce_y(l):
        for r in range(3):
            for h in range(2):
                wait_in(core_in.at[l, h, pl.ds(3 * r, 3)], r_sem["core", l, h, r])
        for p in (2, 1, 3, 0):
            q = (y + p) % 4

            def body(c, carry, q=q):
                rows = pl.ds(pl.multiple_of(c * 32 + q * 8, 8), 8)
                for h in range(2):
                    total = red[l, slot_of(2 * h + core), :, rows, :] + core_in[l, h, :, rows, :]
                    ysend[l, q, c, h] = as_slab(total)
                return carry

            lax.fori_loop(0, 4, body, 0)
            if p:
                for j in near_last:
                    r_sem["y", l, p, j] = pool.take()
                    send(ysend.at[l, q, (z_lo + j) % 4], yrecv.at[l, p - 1, j], at_y(p), r_sem["y", l, p, j])

    def reduce_z(l):
        r_sem["z", l] = pool.take(8)
        for j in near_last:
            c = (z_lo + j) % 4
            for p in range(1, 4):
                wait_in(yrecv.at[l, p - 1, j], r_sem["y", l, p, j])
            for h in range(2):
                total = ysend[l, y, c, h].astype(F32)
                for p in range(3):
                    total = total + yrecv[l, p, j, h].astype(F32)
                total = total.astype(BF)
                zsend[l, j, h] = total
                owner = {"chan": 2 * h + core, "dp": chan, "space": c * 4 + y}
                mine = on_diagonal & (z_hi == h)
                away = jnp.logical_not(mine) if j == 0 else None
                send(zsend.at[l, j, h], zrecv.at[l, z], owner, r_sem["z", l] + z, away)
                if j == 0:

                    @pl.when(mine)
                    def _(total=total):
                        zrecv[l, z] = total

    a_sem = {}
    by_distance = (0, 1, 7, 2, 6, 3, 5, 4)

    def z_from(d):
        other = (z + 8 - d) % 8
        return (other // 4) * 2 + core, other % 4

    def adam(l):
        if l == 1:
            for copy in load_adam:
                copy.wait()
        for q in range(8):
            there = jnp.logical_not(on_diagonal & (z == q))
            pl.when(there)(lambda q=q: wait_in(zrecv.at[l, q], r_sem["z", l] + q))
        grads = zrecv[l, 0].astype(F32)
        for q in range(1, 8):
            grads = grads + zrecv[l, q].astype(F32)
        grads = grads[0:72].reshape(9, 8, 128)
        new_moment = 0.9 * adam_in[1, l] + 0.1 * grads
        new_second = 0.999 * adam_in[2, l] + 0.001 * grads * grads
        corrected = new_moment / (1.0 - 0.9**10)
        scale_term = jnp.sqrt(new_second / (1.0 - 0.999**10)) + 1e-08
        new_master = adam_in[0, l] - 0.01 * corrected / scale_term
        slabs[l, dp, space] = as_slab(new_master)
        here = slabs.at[l, dp, space]
        for p in by_distance[1:]:
            a_sem["z", l, p] = pool.take()
            send(here, here, at_z(p), a_sem["z", l, p])
        to_y(l, 0)
        adam_out[0, l] = new_master
        adam_out[1, l] = new_moment
        adam_out[2, l] = new_second

    def to_y(l, d):
        dp_there, z_there = z_from(d)
        here = slabs.at[l, dp_there, z_there * 4 + y]
        for p in range(1, 4):
            a_sem["y", l, p, d] = pool.take()
            send(here, here, at_y(p), a_sem["y", l, p, d])

    def spread_y(l):
        for d in by_distance[1:]:
            dp_there, z_there = z_from(d)
            wait_in(slabs.at[l, dp_there, z_there * 4 + y], a_sem["z", l, d])
            to_y(l, d)

    def assemble(l, dp_there, z_there):
        for pair in range(2):
            both = [
                slabs[l, dp_there, z_there * 4 + 2 * pair + i].astype(F32)[0:72].reshape(9, 8, 128) for i in range(2)
            ]
            rows = pl.ds(pl.multiple_of(dp_there * 128 + z_there * 32 + pair * 16, 16), 16)
            new_kern[l, :, rows, :] = jnp.concatenate(both, axis=1).astype(BF)
        rows = pl.ds(pl.multiple_of(dp_there * 128 + z_there * 32, 32), 32)
        pltpu.make_async_copy(new_kern.at[l, :, rows, :], kern_out.at[l, :, rows, :], sems.at[a_sem["store", l]]).start()

    def spread_core(l):
        a_sem["store", l] = pool.take()
        for d in by_distance:
            dp_there, z_there = z_from(d)
            for p in range(1, 4):
                wait_in(slabs.at[l, dp_there, z_there * 4 + (y + 4 - p) % 4], a_sem["y", l, p, d])
            a_sem["core", l, d] = pool.take()
            here = slabs.at[l, dp_there, pl.ds(z_there * 4, 4)]
            send(here, here, sibling, a_sem["core", l, d])
            assemble(l, dp_there, z_there)

    def spread_wait(l):
        for d in by_distance:
            dp_there, z_there = z_from(d)
            dp_there = dp_there + 1 - 2 * core
            wait_in(slabs.at[l, dp_there, pl.ds(z_there * 4, 4)], a_sem["core", l, d])
            assemble(l, dp_there, z_there)

    def og_piece(f, i):
        return og_in.at[f, pl.ds(256 * i, 256), :]

    def mg_piece(f, i):
        return gmg.at[(*piece(f, i), pl.ds(0, 128))]

    weights_chan(1)
    gather_own("og", gog, og_piece, 0, pieces)
    rims("mid", mid_in, midpad)
    weights_chan(0)
    hear_half()
    clear_edges()
    load_mid.wait()
    act_inner(1, midpad)
    weights_group(1)
    hear_ring()
    gather_forward("og", gog, 0, (0, 3, 1, 2))
    gather_own("og", gog, og_piece, 1, pieces)
    hear_sibling()
    rims_wait("mid", midpad)
    act_rims(1, midpad)
    weights_group(0)
    rims("x", x_in, xpad)
    load_x.wait()
    act_inner(0, xpad)
    gather_wait("og", gog, 0)
    load_og.wait()
    weights_core(1)
    hear_chan()
    kernel_grad(1, gog, 0)
    gather_forward("og", gog, 1, (0, 3, 1, 2))
    weights_wait(1)
    back_halos(1, gog, 0)
    back_inner(1, gog, 0)
    gather_own("mg", gmg, mg_piece, 0, (1, 2))
    back_outer(1, gog, 0)
    gather_own("mg", gmg, mg_piece, 0, (0, 3))
    gather_wait("og", gog, 1)
    back_halos(1, gog, 1)
    back_inner(1, gog, 1)
    gather_forward("mg", gmg, 0, (1, 2))
    gather_own("mg", gmg, mg_piece, 1, (1, 2))
    back_outer(1, gog, 1)
    gather_forward("mg", gmg, 0, (0, 3))
    gather_own("mg", gmg, mg_piece, 1, (0, 3))
    kernel_grad(1, gog, 1)
    reduce_y(1)
    hear_all()
    weights_core(0)
    rims_wait("x", xpad)
    act_rims(0, xpad)
    weights_wait(0)
    gather_wait("mg", gmg, 0)
    gather_forward("mg", gmg, 1, (1, 2))
    kernel_grad(0, gmg, 0)
    gather_forward("mg", gmg, 1, (0, 3))
    back_halos(0, gmg, 0)
    gather_wait("mg", gmg, 1)
    kernel_grad(0, gmg, 1)
    reduce_z(1)
    reduce_y(0)
    back_halos(0, gmg, 1)
    back_inner(0, gmg, 0)
    back_outer(0, gmg, 0)
    adam(1)
    reduce_z(0)
    back_inner(0, gmg, 1)
    back_outer(0, gmg, 1)
    stores = [load(ig_buf, ig_out)]
    spread_y(1)
    adam(0)
    stores += [load(adam_out.at[k], ref) for k, ref in enumerate((master_out, moment_out, second_out))]
    spread_core(1)
    spread_y(0)
    spread_wait(1)
    spread_core(0)
    spread_wait(0)
    for l in range(2):
        wait_in(new_kern.at[l], a_sem["store", l])
    for copy in stores:
        copy.wait()
    for copy, when in sends:
        if when is None:
            copy.wait_send()
        else:
            pl.when(when)(copy.wait_send)
    assert pool.used <= sems.shape[0], pool.used


def hand_over(ig, kern, master, moment, second, *refs):
    outs, held, sems = refs[:5], refs[5:10], refs[10]
    parts = [(1, (l, pl.ds(3 * r, 3))) for l in range(2) for r in range(3)]
    parts += [(0, (f,)) for f in range(2)] + [(k, (l,)) for k in (2, 3, 4) for l in range(2)]
    ins = (ig, kern, master, moment, second)
    steps = []
    for i, (k, at) in enumerate(parts):
        arrive = pltpu.make_async_copy(ins[k].at[at], held[k].at[at], sems.at[0, i])
        leave = pltpu.make_async_copy(held[k].at[at], outs[k].at[at], sems.at[1, i])
        arrive.start()
        steps.append((arrive, leave))
    for arrive, leave in steps:
        arrive.wait()
        leave.start()
    for arrive, leave in steps:
        leave.wait()


def on_device(section_input, middle, out_grad, kernels, master, moment, second):
    any_space = pl.BlockSpec(memory_space=pl.ANY)
    flat = lambda a: a.reshape(2, PX, 128)
    owned = lambda a: a.reshape(2, 9, 8, 128)
    state = jax.ShapeDtypeStruct((2, 9, 8, 128), F32)
    results = (
        jax.ShapeDtypeStruct((2, PX, 128), BF),
        jax.ShapeDtypeStruct((2, 9, 512, 128), BF),
        state, state, state,
    )
    outs = pl.pallas_call(
        kernel,
        out_shape=results,
        in_specs=[any_space] * 7,
        out_specs=[any_space] * 5,
        scratch_shapes=[
            pltpu.VMEM((2, PX + 256, 128), BF),
            pltpu.VMEM((2, PX + 256, 128), BF),
            pltpu.VMEM((2, PX + 256, 512), BF),
            pltpu.VMEM((2, PX + 256, 512), BF),
            pltpu.VMEM((2, 9, 128, 512), BF),
            pltpu.VMEM((2, 2, 384, PX + 256), BF),
            pltpu.VMEM((2, 4, 9, 128, 128), F32),
            pltpu.VMEM((512, 128), F32),
            pltpu.VMEM((2, 2, 2, 128, 128), F32),
            pltpu.VMEM((2, 2, 2, 128, 128), F32),
            pltpu.VMEM((2, 2, 9, 128, 128), F32),
            pltpu.VMEM((2, 4, 4, 2, SLAB, 128), BF),
            pltpu.VMEM((2, 3, 4, 2, SLAB, 128), BF),
            pltpu.VMEM((2, 4, 2, SLAB, 128), BF),
            pltpu.VMEM((2, 8, SLAB, 128), BF),
            pltpu.VMEM((3, 2, 9, 8, 128), F32),
            pltpu.VMEM((3, 2, 9, 8, 128), F32),
            pltpu.VMEM((2, 4, 16, SLAB, 128), BF),
            pltpu.VMEM((2, 9, 512, 128), BF),
            pltpu.VMEM((2, PX, 128), BF),
            pltpu.SemaphoreType.DMA((SEMS,)),
            pltpu.SemaphoreType.REGULAR((4,)),
        ],
        compiler_params=pltpu.CompilerParams(
            collective_id=0, has_side_effects=True, vmem_limit_bytes=VMEM_LIMIT
        ),
        cost_estimate=pl.CostEstimate(flops=10**10, bytes_accessed=10**7, transcendentals=10**6),
    )(
        flat(section_input), flat(middle), flat(out_grad),
        kernels.reshape(2, 9, 512, 128), owned(master), owned(moment), owned(second),
    )
    outs = pl.pallas_call(
        hand_over,
        out_shape=results,
        in_specs=[any_space] * 5,
        out_specs=[any_space] * 5,
        scratch_shapes=[pltpu.VMEM(r.shape, r.dtype) for r in results] + [pltpu.SemaphoreType.DMA((2, 14))],
    )(*outs)
    shapes = (section_input.shape, kernels.shape, master.shape, master.shape, master.shape)
    return tuple(out.reshape(shape) for out, shape in zip(outs, shapes))


def solution(mesh):
    activation = P("dp", None, "space", None, "chan")
    state = P(None, None, None, ("dp", "space"), "chan")
    weights = P(None, None, None, None, "chan")
    return jax.shard_map(
        on_device,
        mesh=mesh,
        in_specs=(activation, activation, activation, weights, state, state, state),
        out_specs=(activation, weights, state, state, state),
        check_vma=False,
    )
```

```python
import jax
import jax.numpy as jnp
from jax import lax
from jax.experimental import pallas as pl
from jax.experimental.pallas import tpu as pltpu
from jax.sharding import PartitionSpec as P

BF = jnp.bfloat16
F32 = jnp.float32
MESH = pl.DeviceIdType.MESH
PX = 1024
SLAB = 80
SEMS = 520
VMEM_LIMIT = 56 * 1024 * 1024


def sigmoid(v):
    return 1.0 / (1.0 + jnp.exp(-v))


def dsilu(v):
    sig = sigmoid(v)
    return sig * (1.0 + v * (1.0 - sig))


def nt_dot(a, b):
    return lax.dot_general(a, b, (((1,), (1,)), ((), ())), preferred_element_type=F32)


class Sems:
    def __init__(self, ref):
        self.ref = ref
        self.used = 0

    def take(self, count=1):
        base = self.used
        self.used += count
        return base


def kernel(
    x_in, mid_in, og_in, kern, master, moment, second,
    ig_out, kern_out, master_out, moment_out, second_out,
    xpad, midpad, gog, gmg, w, actt, red, back, halo_in, halo_out, core_in,
    ysend, yrecv, zsend, zrecv, adam_in, adam_out, slabs, new_kern, ig_buf, sems, meet,
):
    chan = lax.axis_index("chan")
    dp = lax.axis_index("dp")
    space = lax.axis_index("space")
    z_hi, core = dp // 2, dp % 2
    z_lo, y = space // 4, space % 4
    z = z_hi * 4 + z_lo
    pool = Sems(sems)
    sends = []

    def at_chan(p):
        return {"chan": (chan + p) % 4}

    def at_y(p):
        return {"space": z_lo * 4 + (y + p) % 4}

    def at_z_lo(p):
        return {"space": ((z_lo + p) % 4) * 4 + y}

    def at_z(p):
        other = (z + p) % 8
        return {"dp": (other // 4) * 2 + core, "space": (other % 4) * 4 + y}

    sibling = {"dp": z_hi * 2 + (1 - core)}
    has_prev = space > 0
    has_next = space < 15
    on_diagonal = chan == dp

    def send(src, dst, target, recv_sem, when=None):
        copy = pltpu.make_async_remote_copy(
            src_ref=src, dst_ref=dst, send_sem=sems.at[pool.take()], recv_sem=sems.at[recv_sem],
            device_id=target, device_id_type=MESH,
        )
        if when is None:
            copy.start()
        else:
            pl.when(when)(copy.start)
        sends.append((copy, when))

    def wait_in(dst, sem):
        pltpu.make_async_copy(dst, dst, sems.at[sem]).wait()

    def load(src, dst):
        copy = pltpu.make_async_copy(src, dst, sems.at[pool.take()])
        copy.start()
        return copy

    barrier = pltpu.get_barrier_semaphore()

    def signal(sem, target):
        pl.semaphore_signal(sem, inc=1, device_id=target, device_id_type=MESH)

    prev, nxt = {"space": space - 1}, {"space": space + 1}
    first_z, last_z = z_lo == 0, z_lo == 3
    for p in range(1, 4):
        signal(barrier, at_chan(p))
        signal(barrier, at_y(p))
        signal(barrier, at_z_lo(p))
    signal(barrier, sibling)
    pl.when(has_prev)(lambda: signal(barrier, prev))
    pl.when(has_next)(lambda: signal(barrier, nxt))
    pl.when(first_z)(lambda: signal(barrier, at_z(7)))

    inside = pl.ds(128, PX)
    load_mid = load(mid_in, midpad.at[:, inside, :])
    load_x = load(x_in, xpad.at[:, inside, :])
    load_og = load(og_in, gog.at[:, inside, pl.ds(0, 128)])
    w_parts = ((pl.ds(0, 6), y, at_y), (pl.ds(6, 3), z_lo, at_z_lo))

    def w_rows(index, core=core):
        return pl.ds(core * 64 + index * 16, 16)

    load_w = {
        (l, i): load(
            kern.at[l, taps, pl.ds(chan * 128 + core * 64 + index * 16, 16), :], w.at[l, taps, w_rows(index), pl.ds(0, 128)]
        )
        for l in (1, 0)
        for i, (taps, index, _) in enumerate(w_parts)
    }
    load_adam = [load(ref, adam_in.at[k]) for k, ref in enumerate((master, moment, second))]


    expected = 10 + has_prev.astype(jnp.int32) + has_next.astype(jnp.int32) + last_z.astype(jnp.int32)
    pl.semaphore_wait(barrier, expected)

    def hear_half():
        pl.when(last_z)(lambda: signal(meet.at[0], at_z(1)))

    def hear_ring():
        @pl.when(first_z)
        def _():
            pl.semaphore_wait(meet.at[0], 1)
            for p in range(1, 4):
                signal(meet.at[1], at_z_lo(p))

    def hear_sibling():
        pl.when(jnp.logical_not(first_z))(lambda: pl.semaphore_wait(meet.at[1], 1))
        signal(meet.at[2], sibling)

    def hear_chan():
        pl.semaphore_wait(meet.at[2], 1)
        for p in range(1, 4):
            signal(meet.at[3], at_chan(p))

    def hear_all():
        pl.semaphore_wait(meet.at[3], 3)

    def clear_edges():
        zero_row = jnp.zeros((128, 512), BF)
        for g in (gog, gmg):
            for f in range(2):
                g[f, pl.ds(0, 128), :] = zero_row
                g[f, pl.ds(128 + PX, 128), :] = zero_row

        @pl.when(space == 0)
        def _():
            for pad in (midpad, xpad):
                pad[:, pl.ds(0, 128), :] = jnp.zeros((2, 128, 128), BF)

        @pl.when(space == 15)
        def _():
            for pad in (midpad, xpad):
                pad[:, pl.ds(128 + PX, 128), :] = jnp.zeros((2, 128, 128), BF)

    gathers = {}

    pieces = range(4)

    def piece(f, i):
        return (f, pl.ds(128 + 256 * i, 256))

    def gather_own(name, g, src, f, order):
        sem = gathers.setdefault(name, {})
        for i in order:
            for k in ("left", "right", "far"):
                sem[k, f, i] = pool.take()
        for i, j in zip(order, tuple(order)[::-1]):
            send(src(f, i), g.at[(*piece(f, i), pl.ds(128, 128))], at_chan(1), sem["left", f, i])
            send(src(f, j), g.at[(*piece(f, j), pl.ds(384, 128))], at_chan(3), sem["right", f, j])

    def gather_forward(name, g, f, order):
        sem = gathers[name]
        for i in order:
            k, lanes, target = ("left", 128, at_chan(1)) if i < 2 else ("right", 384, at_chan(3))
            here = g.at[(*piece(f, i), pl.ds(lanes, 128))]
            wait_in(here, sem[k, f, i])
            send(here, g.at[(*piece(f, i), pl.ds(256, 128))], target, sem["far", f, i])

    def gather_wait(name, g, f):
        sem = gathers[name]
        for i in pieces:
            k, lanes = ("right", 384) if i < 2 else ("left", 128)
            wait_in(g.at[(*piece(f, i), pl.ds(lanes, 128))], sem[k, f, i])
            wait_in(g.at[(*piece(f, i), pl.ds(256, 128))], sem["far", f, i])

    w_sem = {}

    def weights_chan(l):
        for i, (taps, index, _) in enumerate(w_parts):
            for p in range(1, 4):
                w_sem["x", l, i, p] = pool.take()
                their = (chan + p) % 4
                send(
                    kern.at[l, taps, pl.ds(their * 128 + core * 64 + index * 16, 16), :],
                    w.at[l, taps, w_rows(index), pl.ds(128 * p, 128)],
                    at_chan(p), w_sem["x", l, i, p],
                )

    def weights_group(l):
        for i, (taps, index, at_peer) in enumerate(w_parts):
            load_w[l, i].wait()
            for p in range(1, 4):
                wait_in(w.at[l, taps, w_rows(index), pl.ds(128 * p, 128)], w_sem["x", l, i, p])
            here = w.at[l, taps, w_rows(index), :]
            for p in (2, 1, 3):
                w_sem["group", l, i, p] = pool.take()
                send(here, here, at_peer(p), w_sem["group", l, i, p])

    def weights_core(l):
        for p in (0, 1, 3, 2):
            for i, (taps, index, _) in enumerate(w_parts):
                here = w.at[l, taps, w_rows((index + 4 - p) % 4), :]
                if p:
                    wait_in(here, w_sem["group", l, i, p])
                w_sem["core", l, i, p] = pool.take()
                send(here, here, sibling, w_sem["core", l, i, p])

    def weights_wait(l):
        for p in (0, 1, 3, 2):
            for i, (taps, index, _) in enumerate(w_parts):
                wait_in(w.at[l, taps, w_rows((index + 4 - p) % 4, 1 - core), :], w_sem["core", l, i, p])

    rim_sem = {}

    def rims(k, src, pad):
        up, down = pool.take(), pool.take()
        rim_sem[k] = (up, down)
        send(src.at[:, pl.ds(PX - 128, 128), :], pad.at[:, pl.ds(0, 128), :], nxt, up, has_next)
        send(src.at[:, pl.ds(0, 128), :], pad.at[:, pl.ds(128 + PX, 128), :], prev, down, has_prev)

    def rims_wait(k, pad):
        up, down = rim_sem[k]
        pl.when(has_prev)(lambda: wait_in(pad.at[:, pl.ds(0, 128), :], up))
        pl.when(has_next)(lambda: wait_in(pad.at[:, pl.ds(128 + PX, 128), :], down))

    def transpose_act(l, pad, first, step, count):
        lane = lax.broadcasted_iota(jnp.int32, (128, 128), 1)

        def body(i, carry):
            f, row = i // count, first + step * (i % count)
            v = pad[f, pl.ds(pl.multiple_of(row * 128, 128), 128), :].astype(F32)
            a = (v * sigmoid(v)).astype(BF).astype(F32).T
            at = pl.ds(pl.multiple_of(row * 128, 128), 128)
            before = jnp.where(lane == 0, 0.0, pltpu.roll(a, 1, 1))
            after = jnp.where(lane == 127, 0.0, pltpu.roll(a, 127, 1))
            actt[l, f, pl.ds(0, 128), at] = before.astype(BF)
            actt[l, f, pl.ds(128, 128), at] = a.astype(BF)
            actt[l, f, pl.ds(256, 128), at] = after.astype(BF)
            return carry

        lax.fori_loop(0, 2 * count, body, 0)

    def act_inner(l, pad):
        transpose_act(l, pad, 1, 1, 8)

    def act_rims(l, pad):
        transpose_act(l, pad, 0, 9, 2)

    def kernel_grad(l, g, f):
        cotangent = g[f, inside, :]
        for r in range(3):
            part = jnp.dot(actt[l, f, :, pl.ds(128 * r, PX)], cotangent, preferred_element_type=F32)
            for k in range(4):
                block = part[:, 128 * k : 128 * k + 128].reshape(3, 128, 128)
                if f:
                    block = block + red[l, k, pl.ds(3 * r, 3)]
                red[l, k, pl.ds(3 * r, 3)] = block
            if f:
                reduce_core(l, r)

    def weight_rows(l, r):
        return w[l, pl.ds(3 * r, 3)].reshape(384, 512)

    def join_taps(acc):
        rows = acc.shape[0]
        col = lax.broadcasted_iota(jnp.int32, (rows, 128), 0) % 128
        first = jnp.where(col == 127, 0.0, pltpu.roll(acc[:, 0:128], rows - 1, 0))
        last = jnp.where(col == 0, 0.0, pltpu.roll(acc[:, 256:384], 1, 0))
        return first + acc[:, 128:256] + last

    halo_sem = {}

    def back_halos(l, g, f):
        up, down = pool.take(), pool.take()
        halo_sem[l, f] = (up, down)
        halo_out[l, f, 0] = join_taps(nt_dot(g[f, pl.ds(128, 128), :], weight_rows(l, 0)))
        halo_out[l, f, 1] = join_taps(nt_dot(g[f, pl.ds(PX, 128), :], weight_rows(l, 2)))
        send(halo_out.at[l, f, 0], halo_in.at[l, f, 1], prev, down, has_prev)
        send(halo_out.at[l, f, 1], halo_in.at[l, f, 0], nxt, up, has_next)

    def back_rows(l, g, f, i):
        start = i * 256
        acc = jnp.zeros((256, 384), F32)
        for r in range(3):
            rows = pl.ds(pl.multiple_of(start + (2 - r) * 128, 128), 256)
            acc = acc + nt_dot(g[f, rows, :], weight_rows(l, r))
        return join_taps(acc)

    def back_inner(l, g, f):
        def body(i, carry):
            finish(l, f, i * 256, back_rows(l, g, f, i))
            return carry

        lax.fori_loop(1, 3, body, 0)

    def back_outer(l, g, f):
        def body(i, carry):
            back[pl.ds(pl.multiple_of(i * 256, 256), 256), :] = back_rows(l, g, f, i * 3)
            return carry

        lax.fori_loop(0, 2, body, 0)
        up, down = halo_sem[l, f]

        @pl.when(has_prev)
        def _():
            wait_in(halo_in.at[l, f, 0], up)
            back[pl.ds(0, 128), :] = back[pl.ds(0, 128), :] + halo_in[l, f, 0]

        @pl.when(has_next)
        def _():
            wait_in(halo_in.at[l, f, 1], down)
            back[pl.ds(384, 128), :] = back[pl.ds(384, 128), :] + halo_in[l, f, 1]

        def close(i, carry):
            finish(l, f, i * 768, back[pl.ds(pl.multiple_of(i * 256, 256), 256), :])
            return carry

        lax.fori_loop(0, 2, close, 0)

    def finish(l, f, start, total):
        rows = pl.ds(pl.multiple_of(start, 128), 256)
        padded = pl.ds(pl.multiple_of(start + 128, 128), 256)
        if l:
            v = midpad[f, padded, :].astype(F32)
            gmg[f, padded, pl.ds(0, 128)] = (total * dsilu(v)).astype(BF)
        else:
            v = xpad[f, padded, :].astype(F32)
            og = gog[f, padded, pl.ds(0, 128)].astype(F32)
            ig_buf[f, rows, :] = (og + total * dsilu(v)).astype(BF)

    r_sem = {}

    def slot_of(block):
        return (chan + 4 - block) % 4

    def reduce_core(l, r):
        for h in range(2):
            r_sem["core", l, h, r] = pool.take()
            taps = pl.ds(3 * r, 3)
            send(red.at[l, slot_of(2 * h + 1 - core), taps], core_in.at[l, h, taps], sibling, r_sem["core", l, h, r])

    def as_slab(v):
        return jnp.concatenate([v.reshape(72, 128), jnp.zeros((8, 128), F32)], axis=0).astype(BF)

    near_last = (2, 3, 1, 0)
    z_first = z_lo + 2 * ((chan // 2 + z_hi) % 2)

    def reduce_y(l):
        for r in range(3):
            for h in range(2):
                wait_in(core_in.at[l, h, pl.ds(3 * r, 3)], r_sem["core", l, h, r])
        for j in near_last:
            c = (z_first + j) % 4

            def body(q, carry, c=c):
                rows = pl.ds(pl.multiple_of(c * 32 + q * 8, 8), 8)
                for h in range(2):
                    total = red[l, slot_of(2 * h + core), :, rows, :] + core_in[l, h, :, rows, :]
                    ysend[l, q, c, h] = as_slab(total)
                return carry

            lax.fori_loop(0, 4, body, 0)
            for p in (2, 1, 3):
                r_sem["y", l, p, j] = pool.take()
                send(ysend.at[l, (y + p) % 4, c], yrecv.at[l, p - 1, j], at_y(p), r_sem["y", l, p, j])

    def reduce_z(l):
        r_sem["z", l] = pool.take(8)
        for j in near_last:
            c = (z_first + j) % 4
            for p in range(1, 4):
                wait_in(yrecv.at[l, p - 1, j], r_sem["y", l, p, j])
            for h in range(2):
                total = ysend[l, y, c, h].astype(F32)
                for p in range(3):
                    total = total + yrecv[l, p, j, h].astype(F32)
                total = total.astype(BF)
                zsend[l, j, h] = total
                owner = {"chan": 2 * h + core, "dp": chan, "space": c * 4 + y}
                mine = on_diagonal & (z_hi == h)
                away = jnp.logical_not(mine) if j == 0 else None
                send(zsend.at[l, j, h], zrecv.at[l, z], owner, r_sem["z", l] + z, away)
                if j == 0:

                    @pl.when(mine)
                    def _(total=total):
                        zrecv[l, z] = total

    a_sem = {}
    by_distance = (0, 1, 7, 2, 6, 3, 5, 4)

    def z_from(d):
        other = (z + 8 - d) % 8
        return (other // 4) * 2 + core, other % 4

    def adam(l):
        if l == 1:
            for copy in load_adam:
                copy.wait()
        for q in range(8):
            there = jnp.logical_not(on_diagonal & (z == q))
            pl.when(there)(lambda q=q: wait_in(zrecv.at[l, q], r_sem["z", l] + q))
        grads = zrecv[l, 0].astype(F32)
        for q in range(1, 8):
            grads = grads + zrecv[l, q].astype(F32)
        grads = grads[0:72].reshape(9, 8, 128)
        new_moment = 0.9 * adam_in[1, l] + 0.1 * grads
        new_second = 0.999 * adam_in[2, l] + 0.001 * grads * grads
        corrected = new_moment / (1.0 - 0.9**10)
        scale_term = jnp.sqrt(new_second / (1.0 - 0.999**10)) + 1e-08
        new_master = adam_in[0, l] - 0.01 * corrected / scale_term
        slabs[l, dp, space] = as_slab(new_master)
        here = slabs.at[l, dp, space]
        for p in by_distance[1:]:
            a_sem["z", l, p] = pool.take()
            send(here, here, at_z(p), a_sem["z", l, p])
        adam_out[0, l] = new_master
        adam_out[1, l] = new_moment
        adam_out[2, l] = new_second

    def to_y(l, d):
        dp_there, z_there = z_from(d)
        here = slabs.at[l, dp_there, z_there * 4 + y]
        for p in range(1, 4):
            a_sem["y", l, p, d] = pool.take()
            send(here, here, at_y(p), a_sem["y", l, p, d])

    def spread_y(l):
        for d in by_distance:
            if d:
                dp_there, z_there = z_from(d)
                wait_in(slabs.at[l, dp_there, z_there * 4 + y], a_sem["z", l, d])
            to_y(l, d)

    def assemble(l, dp_there, z_there):
        for pair in range(2):
            both = [
                slabs[l, dp_there, z_there * 4 + 2 * pair + i].astype(F32)[0:72].reshape(9, 8, 128) for i in range(2)
            ]
            rows = pl.ds(pl.multiple_of(dp_there * 128 + z_there * 32 + pair * 16, 16), 16)
            new_kern[l, :, rows, :] = jnp.concatenate(both, axis=1).astype(BF)
        rows = pl.ds(pl.multiple_of(dp_there * 128 + z_there * 32, 32), 32)
        pltpu.make_async_copy(new_kern.at[l, :, rows, :], kern_out.at[l, :, rows, :], sems.at[a_sem["store", l]]).start()

    def spread_core(l):
        a_sem["store", l] = pool.take()
        for d in by_distance:
            dp_there, z_there = z_from(d)
            for p in range(1, 4):
                wait_in(slabs.at[l, dp_there, z_there * 4 + (y + 4 - p) % 4], a_sem["y", l, p, d])
            a_sem["core", l, d] = pool.take()
            here = slabs.at[l, dp_there, pl.ds(z_there * 4, 4)]
            send(here, here, sibling, a_sem["core", l, d])
            assemble(l, dp_there, z_there)

    def spread_wait(l):
        for d in by_distance:
            dp_there, z_there = z_from(d)
            dp_there = dp_there + 1 - 2 * core
            wait_in(slabs.at[l, dp_there, pl.ds(z_there * 4, 4)], a_sem["core", l, d])
            assemble(l, dp_there, z_there)

    def og_piece(f, i):
        return og_in.at[f, pl.ds(256 * i, 256), :]

    def mg_piece(f, i):
        return gmg.at[(*piece(f, i), pl.ds(0, 128))]

    weights_chan(1)
    gather_own("og", gog, og_piece, 0, pieces)
    rims("mid", mid_in, midpad)
    weights_chan(0)
    hear_half()
    clear_edges()
    load_mid.wait()
    act_inner(1, midpad)
    weights_group(1)
    hear_ring()
    gather_forward("og", gog, 0, (0, 3, 1, 2))
    gather_own("og", gog, og_piece, 1, pieces)
    hear_sibling()
    rims_wait("mid", midpad)
    act_rims(1, midpad)
    weights_group(0)
    rims("x", x_in, xpad)
    load_x.wait()
    act_inner(0, xpad)
    gather_wait("og", gog, 0)
    load_og.wait()
    weights_core(1)
    hear_chan()
    kernel_grad(1, gog, 0)
    gather_forward("og", gog, 1, (0, 3, 1, 2))
    weights_wait(1)
    back_halos(1, gog, 0)
    back_inner(1, gog, 0)
    gather_own("mg", gmg, mg_piece, 0, (1, 2))
    back_outer(1, gog, 0)
    gather_own("mg", gmg, mg_piece, 0, (0, 3))
    gather_wait("og", gog, 1)
    back_halos(1, gog, 1)
    back_inner(1, gog, 1)
    kernel_grad(1, gog, 1)
    gather_forward("mg", gmg, 0, (1, 2))
    gather_own("mg", gmg, mg_piece, 1, (1, 2))
    back_outer(1, gog, 1)
    gather_forward("mg", gmg, 0, (0, 3))
    gather_own("mg", gmg, mg_piece, 1, (0, 3))
    reduce_y(1)
    hear_all()
    weights_core(0)
    rims_wait("x", xpad)
    act_rims(0, xpad)
    weights_wait(0)
    gather_wait("mg", gmg, 0)
    gather_forward("mg", gmg, 1, (1, 2))
    kernel_grad(0, gmg, 0)
    gather_forward("mg", gmg, 1, (0, 3))
    back_halos(0, gmg, 0)
    reduce_z(1)
    gather_wait("mg", gmg, 1)
    kernel_grad(0, gmg, 1)
    reduce_y(0)
    adam(1)
    back_halos(0, gmg, 1)
    back_inner(0, gmg, 0)
    back_outer(0, gmg, 0)
    back_inner(0, gmg, 1)
    reduce_z(0)
    spread_y(1)
    back_outer(0, gmg, 1)
    stores = [load(ig_buf, ig_out)]
    adam(0)
    stores += [load(adam_out.at[k], ref) for k, ref in enumerate((master_out, moment_out, second_out))]
    spread_core(1)
    spread_y(0)
    spread_wait(1)
    spread_core(0)
    spread_wait(0)
    for l in range(2):
        wait_in(new_kern.at[l], a_sem["store", l])
    for copy in stores:
        copy.wait()
    for copy, when in sends:
        if when is None:
            copy.wait_send()
        else:
            pl.when(when)(copy.wait_send)
    assert pool.used <= sems.shape[0], pool.used


def hand_over(ig, kern, master, moment, second, *refs):
    outs, held, sems = refs[:5], refs[5:10], refs[10]
    parts = [(1, (l, pl.ds(3 * r, 3))) for l in range(2) for r in range(3)]
    parts += [(0, (f,)) for f in range(2)] + [(k, (l,)) for k in (2, 3, 4) for l in range(2)]
    ins = (ig, kern, master, moment, second)
    steps = []
    for i, (k, at) in enumerate(parts):
        arrive = pltpu.make_async_copy(ins[k].at[at], held[k].at[at], sems.at[0, i])
        leave = pltpu.make_async_copy(held[k].at[at], outs[k].at[at], sems.at[1, i])
        arrive.start()
        steps.append((arrive, leave))
    for arrive, leave in steps:
        arrive.wait()
        leave.start()
    for arrive, leave in steps:
        leave.wait()


def on_device(section_input, middle, out_grad, kernels, master, moment, second):
    any_space = pl.BlockSpec(memory_space=pl.ANY)
    flat = lambda a: a.reshape(2, PX, 128)
    owned = lambda a: a.reshape(2, 9, 8, 128)
    state = jax.ShapeDtypeStruct((2, 9, 8, 128), F32)
    results = (
        jax.ShapeDtypeStruct((2, PX, 128), BF),
        jax.ShapeDtypeStruct((2, 9, 512, 128), BF),
        state, state, state,
    )
    outs = pl.pallas_call(
        kernel,
        out_shape=results,
        in_specs=[any_space] * 7,
        out_specs=[any_space] * 5,
        scratch_shapes=[
            pltpu.VMEM((2, PX + 256, 128), BF),
            pltpu.VMEM((2, PX + 256, 128), BF),
            pltpu.VMEM((2, PX + 256, 512), BF),
            pltpu.VMEM((2, PX + 256, 512), BF),
            pltpu.VMEM((2, 9, 128, 512), BF),
            pltpu.VMEM((2, 2, 384, PX + 256), BF),
            pltpu.VMEM((2, 4, 9, 128, 128), F32),
            pltpu.VMEM((512, 128), F32),
            pltpu.VMEM((2, 2, 2, 128, 128), F32),
            pltpu.VMEM((2, 2, 2, 128, 128), F32),
            pltpu.VMEM((2, 2, 9, 128, 128), F32),
            pltpu.VMEM((2, 4, 4, 2, SLAB, 128), BF),
            pltpu.VMEM((2, 3, 4, 2, SLAB, 128), BF),
            pltpu.VMEM((2, 4, 2, SLAB, 128), BF),
            pltpu.VMEM((2, 8, SLAB, 128), BF),
            pltpu.VMEM((3, 2, 9, 8, 128), F32),
            pltpu.VMEM((3, 2, 9, 8, 128), F32),
            pltpu.VMEM((2, 4, 16, SLAB, 128), BF),
            pltpu.VMEM((2, 9, 512, 128), BF),
            pltpu.VMEM((2, PX, 128), BF),
            pltpu.SemaphoreType.DMA((SEMS,)),
            pltpu.SemaphoreType.REGULAR((4,)),
        ],
        compiler_params=pltpu.CompilerParams(
            collective_id=0, has_side_effects=True, vmem_limit_bytes=VMEM_LIMIT
        ),
        cost_estimate=pl.CostEstimate(flops=10**10, bytes_accessed=10**7, transcendentals=10**6),
    )(
        flat(section_input), flat(middle), flat(out_grad),
        kernels.reshape(2, 9, 512, 128), owned(master), owned(moment), owned(second),
    )
    outs = pl.pallas_call(
        hand_over,
        out_shape=results,
        in_specs=[any_space] * 5,
        out_specs=[any_space] * 5,
        scratch_shapes=[pltpu.VMEM(r.shape, r.dtype) for r in results] + [pltpu.SemaphoreType.DMA((2, 14))],
    )(*outs)
    shapes = (section_input.shape, kernels.shape, master.shape, master.shape, master.shape)
    return tuple(out.reshape(shape) for out, shape in zip(outs, shapes))


def solution(mesh):
    activation = P("dp", None, "space", None, "chan")
    state = P(None, None, None, ("dp", "space"), "chan")
    weights = P(None, None, None, None, "chan")
    return jax.shard_map(
        on_device,
        mesh=mesh,
        in_specs=(activation, activation, activation, weights, state, state, state),
        out_specs=(activation, weights, state, state, state),
        check_vma=False,
    )
```

```python
import jax
import jax.numpy as jnp
from jax import lax
from jax.experimental import pallas as pl
from jax.experimental.pallas import tpu as pltpu
from jax.sharding import PartitionSpec as P

BF = jnp.bfloat16
F32 = jnp.float32
MESH = pl.DeviceIdType.MESH
PX = 1024
SLAB = 80
SEMS = 520
VMEM_LIMIT = 56 * 1024 * 1024


def sigmoid(v):
    return 1.0 / (1.0 + jnp.exp(-v))


def dsilu(v):
    sig = sigmoid(v)
    return sig * (1.0 + v * (1.0 - sig))


def nt_dot(a, b):
    return lax.dot_general(a, b, (((1,), (1,)), ((), ())), preferred_element_type=F32)


class Sems:
    def __init__(self, ref):
        self.ref = ref
        self.used = 0

    def take(self, count=1):
        base = self.used
        self.used += count
        return base


def kernel(
    x_in, mid_in, og_in, kern, master, moment, second,
    ig_out, kern_out, master_out, moment_out, second_out,
    xpad, midpad, gog, gmg, w, actt, red, back, halo_in, halo_out, core_in,
    ysend, yrecv, zsend, zrecv, adam_in, adam_out, slabs, new_kern, ig_buf, sems, meet,
):
    chan = lax.axis_index("chan")
    dp = lax.axis_index("dp")
    space = lax.axis_index("space")
    z_hi, core = dp // 2, dp % 2
    z_lo, y = space // 4, space % 4
    z = z_hi * 4 + z_lo
    pool = Sems(sems)
    sends = []

    def at_chan(p):
        return {"chan": (chan + p) % 4}

    def at_y(p):
        return {"space": z_lo * 4 + (y + p) % 4}

    def at_z_lo(p):
        return {"space": ((z_lo + p) % 4) * 4 + y}

    def at_z(p):
        other = (z + p) % 8
        return {"dp": (other // 4) * 2 + core, "space": (other % 4) * 4 + y}

    sibling = {"dp": z_hi * 2 + (1 - core)}
    has_prev = space > 0
    has_next = space < 15
    on_diagonal = chan == dp

    def send(src, dst, target, recv_sem, when=None):
        copy = pltpu.make_async_remote_copy(
            src_ref=src, dst_ref=dst, send_sem=sems.at[pool.take()], recv_sem=sems.at[recv_sem],
            device_id=target, device_id_type=MESH,
        )
        if when is None:
            copy.start()
        else:
            pl.when(when)(copy.start)
        sends.append((copy, when))

    def wait_in(dst, sem):
        pltpu.make_async_copy(dst, dst, sems.at[sem]).wait()

    def load(src, dst):
        copy = pltpu.make_async_copy(src, dst, sems.at[pool.take()])
        copy.start()
        return copy

    barrier = pltpu.get_barrier_semaphore()

    def signal(sem, target):
        pl.semaphore_signal(sem, inc=1, device_id=target, device_id_type=MESH)

    prev, nxt = {"space": space - 1}, {"space": space + 1}
    first_z, last_z = z_lo == 0, z_lo == 3
    for p in range(1, 4):
        signal(barrier, at_chan(p))
        signal(barrier, at_y(p))
        signal(barrier, at_z_lo(p))
    signal(barrier, sibling)
    pl.when(has_prev)(lambda: signal(barrier, prev))
    pl.when(has_next)(lambda: signal(barrier, nxt))
    pl.when(first_z)(lambda: signal(barrier, at_z(7)))

    inside = pl.ds(128, PX)
    load_mid = load(mid_in, midpad.at[:, inside, :])
    load_x = load(x_in, xpad.at[:, inside, :])
    load_og = load(og_in, gog.at[:, inside, pl.ds(0, 128)])
    w_parts = ((pl.ds(0, 6), y, at_y), (pl.ds(6, 3), z_lo, at_z_lo))

    def w_rows(index, core=core):
        return pl.ds(core * 64 + index * 16, 16)

    load_w = {
        (l, i): load(
            kern.at[l, taps, pl.ds(chan * 128 + core * 64 + index * 16, 16), :], w.at[l, taps, w_rows(index), pl.ds(0, 128)]
        )
        for l in (1, 0)
        for i, (taps, index, _) in enumerate(w_parts)
    }
    load_adam = [load(ref, adam_in.at[k]) for k, ref in enumerate((master, moment, second))]


    expected = 10 + has_prev.astype(jnp.int32) + has_next.astype(jnp.int32) + last_z.astype(jnp.int32)
    pl.semaphore_wait(barrier, expected)

    def hear_half():
        pl.when(last_z)(lambda: signal(meet.at[0], at_z(1)))

    def hear_ring():
        @pl.when(first_z)
        def _():
            pl.semaphore_wait(meet.at[0], 1)
            for p in range(1, 4):
                signal(meet.at[1], at_z_lo(p))

    def hear_sibling():
        pl.when(jnp.logical_not(first_z))(lambda: pl.semaphore_wait(meet.at[1], 1))
        signal(meet.at[2], sibling)

    def hear_chan():
        pl.semaphore_wait(meet.at[2], 1)
        for p in range(1, 4):
            signal(meet.at[3], at_chan(p))

    def hear_all():
        pl.semaphore_wait(meet.at[3], 3)

    def clear_edges():
        zero_row = jnp.zeros((128, 512), BF)
        for g in (gog, gmg):
            for f in range(2):
                g[f, pl.ds(0, 128), :] = zero_row
                g[f, pl.ds(128 + PX, 128), :] = zero_row

        @pl.when(space == 0)
        def _():
            for pad in (midpad, xpad):
                pad[:, pl.ds(0, 128), :] = jnp.zeros((2, 128, 128), BF)

        @pl.when(space == 15)
        def _():
            for pad in (midpad, xpad):
                pad[:, pl.ds(128 + PX, 128), :] = jnp.zeros((2, 128, 128), BF)

    gathers = {}

    pieces = range(4)

    def piece(f, i):
        return (f, pl.ds(128 + 256 * i, 256))

    def gather_own(name, g, src, f, order):
        sem = gathers.setdefault(name, {})
        for i in order:
            for k in ("left", "right", "far"):
                sem[k, f, i] = pool.take()
        for i, j in zip(order, tuple(order)[::-1]):
            send(src(f, i), g.at[(*piece(f, i), pl.ds(128, 128))], at_chan(1), sem["left", f, i])
            send(src(f, j), g.at[(*piece(f, j), pl.ds(384, 128))], at_chan(3), sem["right", f, j])

    def gather_forward(name, g, f, order):
        sem = gathers[name]
        for i in order:
            k, lanes, target = ("left", 128, at_chan(1)) if i < 2 else ("right", 384, at_chan(3))
            here = g.at[(*piece(f, i), pl.ds(lanes, 128))]
            wait_in(here, sem[k, f, i])
            send(here, g.at[(*piece(f, i), pl.ds(256, 128))], target, sem["far", f, i])

    def gather_wait(name, g, f):
        sem = gathers[name]
        for i in pieces:
            k, lanes = ("right", 384) if i < 2 else ("left", 128)
            wait_in(g.at[(*piece(f, i), pl.ds(lanes, 128))], sem[k, f, i])
            wait_in(g.at[(*piece(f, i), pl.ds(256, 128))], sem["far", f, i])

    w_sem = {}

    def weights_chan(l):
        for i, (taps, index, _) in enumerate(w_parts):
            for p in range(1, 4):
                w_sem["x", l, i, p] = pool.take()
                their = (chan + p) % 4
                send(
                    kern.at[l, taps, pl.ds(their * 128 + core * 64 + index * 16, 16), :],
                    w.at[l, taps, w_rows(index), pl.ds(128 * p, 128)],
                    at_chan(p), w_sem["x", l, i, p],
                )

    def weights_group(l):
        for i, (taps, index, at_peer) in enumerate(w_parts):
            load_w[l, i].wait()
            for p in range(1, 4):
                wait_in(w.at[l, taps, w_rows(index), pl.ds(128 * p, 128)], w_sem["x", l, i, p])
            here = w.at[l, taps, w_rows(index), :]
            for p in (2, 1, 3):
                w_sem["group", l, i, p] = pool.take()
                send(here, here, at_peer(p), w_sem["group", l, i, p])

    def weights_core(l):
        for p in (0, 1, 3, 2):
            for i, (taps, index, _) in enumerate(w_parts):
                here = w.at[l, taps, w_rows((index + 4 - p) % 4), :]
                if p:
                    wait_in(here, w_sem["group", l, i, p])
                w_sem["core", l, i, p] = pool.take()
                send(here, here, sibling, w_sem["core", l, i, p])

    def weights_wait(l):
        for p in (0, 1, 3, 2):
            for i, (taps, index, _) in enumerate(w_parts):
                wait_in(w.at[l, taps, w_rows((index + 4 - p) % 4, 1 - core), :], w_sem["core", l, i, p])

    rim_sem = {}

    def rims(k, src, pad):
        up, down = pool.take(), pool.take()
        rim_sem[k] = (up, down)
        send(src.at[:, pl.ds(PX - 128, 128), :], pad.at[:, pl.ds(0, 128), :], nxt, up, has_next)
        send(src.at[:, pl.ds(0, 128), :], pad.at[:, pl.ds(128 + PX, 128), :], prev, down, has_prev)

    def rims_wait(k, pad):
        up, down = rim_sem[k]
        pl.when(has_prev)(lambda: wait_in(pad.at[:, pl.ds(0, 128), :], up))
        pl.when(has_next)(lambda: wait_in(pad.at[:, pl.ds(128 + PX, 128), :], down))

    def transpose_act(l, pad, first, step, count):
        lane = lax.broadcasted_iota(jnp.int32, (128, 128), 1)

        def body(i, carry):
            f, row = i // count, first + step * (i % count)
            v = pad[f, pl.ds(pl.multiple_of(row * 128, 128), 128), :].astype(F32)
            a = (v * sigmoid(v)).astype(BF).astype(F32).T
            at = pl.ds(pl.multiple_of(row * 128, 128), 128)
            before = jnp.where(lane == 0, 0.0, pltpu.roll(a, 1, 1))
            after = jnp.where(lane == 127, 0.0, pltpu.roll(a, 127, 1))
            actt[l, f, pl.ds(0, 128), at] = before.astype(BF)
            actt[l, f, pl.ds(128, 128), at] = a.astype(BF)
            actt[l, f, pl.ds(256, 128), at] = after.astype(BF)
            return carry

        lax.fori_loop(0, 2 * count, body, 0)

    def act_inner(l, pad):
        transpose_act(l, pad, 1, 1, 8)

    def act_rims(l, pad):
        transpose_act(l, pad, 0, 9, 2)

    def kernel_grad(l, g, f):
        cotangent = g[f, inside, :]
        for r in range(3):
            part = jnp.dot(actt[l, f, :, pl.ds(128 * r, PX)], cotangent, preferred_element_type=F32)
            for k in range(4):
                block = part[:, 128 * k : 128 * k + 128].reshape(3, 128, 128)
                if f:
                    block = block + red[l, k, pl.ds(3 * r, 3)]
                red[l, k, pl.ds(3 * r, 3)] = block
            if f:
                reduce_core(l, r)

    def weight_rows(l, r):
        return w[l, pl.ds(3 * r, 3)].reshape(384, 512)

    def join_taps(acc):
        rows = acc.shape[0]
        col = lax.broadcasted_iota(jnp.int32, (rows, 128), 0) % 128
        first = jnp.where(col == 127, 0.0, pltpu.roll(acc[:, 0:128], rows - 1, 0))
        last = jnp.where(col == 0, 0.0, pltpu.roll(acc[:, 256:384], 1, 0))
        return first + acc[:, 128:256] + last

    halo_sem = {}

    def back_halos(l, g, f):
        up, down = pool.take(), pool.take()
        halo_sem[l, f] = (up, down)
        halo_out[l, f, 0] = join_taps(nt_dot(g[f, pl.ds(128, 128), :], weight_rows(l, 0)))
        halo_out[l, f, 1] = join_taps(nt_dot(g[f, pl.ds(PX, 128), :], weight_rows(l, 2)))
        send(halo_out.at[l, f, 0], halo_in.at[l, f, 1], prev, down, has_prev)
        send(halo_out.at[l, f, 1], halo_in.at[l, f, 0], nxt, up, has_next)

    def back_rows(l, g, f, i):
        start = i * 256
        acc = jnp.zeros((256, 384), F32)
        for r in range(3):
            rows = pl.ds(pl.multiple_of(start + (2 - r) * 128, 128), 256)
            acc = acc + nt_dot(g[f, rows, :], weight_rows(l, r))
        return join_taps(acc)

    def back_inner(l, g, f):
        def body(i, carry):
            finish(l, f, i * 256, back_rows(l, g, f, i))
            return carry

        lax.fori_loop(1, 3, body, 0)

    def back_outer(l, g, f):
        def body(i, carry):
            back[pl.ds(pl.multiple_of(i * 256, 256), 256), :] = back_rows(l, g, f, i * 3)
            return carry

        lax.fori_loop(0, 2, body, 0)
        up, down = halo_sem[l, f]

        @pl.when(has_prev)
        def _():
            wait_in(halo_in.at[l, f, 0], up)
            back[pl.ds(0, 128), :] = back[pl.ds(0, 128), :] + halo_in[l, f, 0]

        @pl.when(has_next)
        def _():
            wait_in(halo_in.at[l, f, 1], down)
            back[pl.ds(384, 128), :] = back[pl.ds(384, 128), :] + halo_in[l, f, 1]

        def close(i, carry):
            finish(l, f, i * 768, back[pl.ds(pl.multiple_of(i * 256, 256), 256), :])
            return carry

        lax.fori_loop(0, 2, close, 0)

    def finish(l, f, start, total):
        rows = pl.ds(pl.multiple_of(start, 128), 256)
        padded = pl.ds(pl.multiple_of(start + 128, 128), 256)
        if l:
            v = midpad[f, padded, :].astype(F32)
            gmg[f, padded, pl.ds(0, 128)] = (total * dsilu(v)).astype(BF)
        else:
            v = xpad[f, padded, :].astype(F32)
            og = gog[f, padded, pl.ds(0, 128)].astype(F32)
            ig_buf[f, rows, :] = (og + total * dsilu(v)).astype(BF)

    r_sem = {}

    def slot_of(block):
        return (chan + 4 - block) % 4

    def reduce_core(l, r):
        for h in range(2):
            r_sem["core", l, h, r] = pool.take()
            taps = pl.ds(3 * r, 3)
            send(red.at[l, slot_of(2 * h + 1 - core), taps], core_in.at[l, h, taps], sibling, r_sem["core", l, h, r])

    def as_slab(v):
        return jnp.concatenate([v.reshape(72, 128), jnp.zeros((8, 128), F32)], axis=0).astype(BF)

    near_last = (2, 3, 1, 0)
    z_first = z_lo + 2 * ((chan // 2 + z_hi) % 2)

    def reduce_y(l):
        for r in range(3):
            for h in range(2):
                wait_in(core_in.at[l, h, pl.ds(3 * r, 3)], r_sem["core", l, h, r])
        for j in near_last:
            c = (z_first + j) % 4

            def body(q, carry, c=c):
                rows = pl.ds(pl.multiple_of(c * 32 + q * 8, 8), 8)
                for h in range(2):
                    total = red[l, slot_of(2 * h + core), :, rows, :] + core_in[l, h, :, rows, :]
                    ysend[l, q, c, h] = as_slab(total)
                return carry

            lax.fori_loop(0, 4, body, 0)
            for p in (2, 1, 3):
                r_sem["y", l, p, j] = pool.take()
                send(ysend.at[l, (y + p) % 4, c], yrecv.at[l, p - 1, j], at_y(p), r_sem["y", l, p, j])

    def reduce_z(l):
        r_sem["z", l] = pool.take(8)
        for j in near_last:
            c = (z_first + j) % 4
            for p in range(1, 4):
                wait_in(yrecv.at[l, p - 1, j], r_sem["y", l, p, j])
            for h in range(2):
                total = ysend[l, y, c, h].astype(F32)
                for p in range(3):
                    total = total + yrecv[l, p, j, h].astype(F32)
                total = total.astype(BF)
                zsend[l, j, h] = total
                owner = {"chan": 2 * h + core, "dp": chan, "space": c * 4 + y}
                mine = on_diagonal & (z_hi == h)
                away = jnp.logical_not(mine) if j == 0 else None
                send(zsend.at[l, j, h], zrecv.at[l, z], owner, r_sem["z", l] + z, away)
                if j == 0:

                    @pl.when(mine)
                    def _(total=total):
                        zrecv[l, z] = total

    a_sem = {}
    by_distance = (0, 1, 7, 2, 6, 3, 5, 4)

    def z_from(d):
        other = (z + 8 - d) % 8
        return (other // 4) * 2 + core, other % 4

    def adam(l):
        if l == 1:
            for copy in load_adam:
                copy.wait()
        for q in range(8):
            there = jnp.logical_not(on_diagonal & (z == q))
            pl.when(there)(lambda q=q: wait_in(zrecv.at[l, q], r_sem["z", l] + q))
        grads = zrecv[l, 0].astype(F32)
        for q in range(1, 8):
            grads = grads + zrecv[l, q].astype(F32)
        grads = grads[0:72].reshape(9, 8, 128)
        new_moment = 0.9 * adam_in[1, l] + 0.1 * grads
        new_second = 0.999 * adam_in[2, l] + 0.001 * grads * grads
        corrected = new_moment / (1.0 - 0.9**10)
        scale_term = jnp.sqrt(new_second / (1.0 - 0.999**10)) + 1e-08
        new_master = adam_in[0, l] - 0.01 * corrected / scale_term
        slabs[l, dp, space] = as_slab(new_master)
        here = slabs.at[l, dp, space]
        for p in by_distance[1:]:
            a_sem["z", l, p] = pool.take()
            send(here, here, at_z(p), a_sem["z", l, p])
        adam_out[0, l] = new_master
        adam_out[1, l] = new_moment
        adam_out[2, l] = new_second

    def to_y(l, d):
        dp_there, z_there = z_from(d)
        here = slabs.at[l, dp_there, z_there * 4 + y]
        for p in range(1, 4):
            a_sem["y", l, p, d] = pool.take()
            send(here, here, at_y(p), a_sem["y", l, p, d])

    def spread_y(l):
        for d in by_distance:
            if d:
                dp_there, z_there = z_from(d)
                wait_in(slabs.at[l, dp_there, z_there * 4 + y], a_sem["z", l, d])
            to_y(l, d)

    def assemble(l, dp_there, z_there):
        for pair in range(2):
            both = [
                slabs[l, dp_there, z_there * 4 + 2 * pair + i].astype(F32)[0:72].reshape(9, 8, 128) for i in range(2)
            ]
            rows = pl.ds(pl.multiple_of(dp_there * 128 + z_there * 32 + pair * 16, 16), 16)
            new_kern[l, :, rows, :] = jnp.concatenate(both, axis=1).astype(BF)
        rows = pl.ds(pl.multiple_of(dp_there * 128 + z_there * 32, 32), 32)
        pltpu.make_async_copy(new_kern.at[l, :, rows, :], kern_out.at[l, :, rows, :], sems.at[a_sem["store", l]]).start()

    def spread_core(l):
        a_sem["store", l] = pool.take()
        for d in by_distance:
            dp_there, z_there = z_from(d)
            for p in range(1, 4):
                wait_in(slabs.at[l, dp_there, z_there * 4 + (y + 4 - p) % 4], a_sem["y", l, p, d])
            a_sem["core", l, d] = pool.take()
            here = slabs.at[l, dp_there, pl.ds(z_there * 4, 4)]
            send(here, here, sibling, a_sem["core", l, d])
            assemble(l, dp_there, z_there)

    def spread_wait(l):
        for d in by_distance:
            dp_there, z_there = z_from(d)
            dp_there = dp_there + 1 - 2 * core
            wait_in(slabs.at[l, dp_there, pl.ds(z_there * 4, 4)], a_sem["core", l, d])
            assemble(l, dp_there, z_there)

    def og_piece(f, i):
        return og_in.at[f, pl.ds(256 * i, 256), :]

    def mg_piece(f, i):
        return gmg.at[(*piece(f, i), pl.ds(0, 128))]

    weights_chan(1)
    gather_own("og", gog, og_piece, 0, pieces)
    rims("mid", mid_in, midpad)
    weights_chan(0)
    hear_half()
    clear_edges()
    load_mid.wait()
    act_inner(1, midpad)
    weights_group(1)
    hear_ring()
    gather_forward("og", gog, 0, (0, 3, 1, 2))
    gather_own("og", gog, og_piece, 1, pieces)
    hear_sibling()
    rims_wait("mid", midpad)
    act_rims(1, midpad)
    weights_group(0)
    rims("x", x_in, xpad)
    load_x.wait()
    act_inner(0, xpad)
    gather_wait("og", gog, 0)
    load_og.wait()
    weights_core(1)
    hear_chan()
    kernel_grad(1, gog, 0)
    gather_forward("og", gog, 1, (0, 3, 1, 2))
    weights_wait(1)
    back_halos(1, gog, 0)
    back_inner(1, gog, 0)
    gather_own("mg", gmg, mg_piece, 0, (1, 2))
    back_outer(1, gog, 0)
    gather_own("mg", gmg, mg_piece, 0, (0, 3))
    gather_wait("og", gog, 1)
    back_halos(1, gog, 1)
    back_inner(1, gog, 1)
    gather_forward("mg", gmg, 0, (1, 2))
    gather_own("mg", gmg, mg_piece, 1, (1, 2))
    kernel_grad(1, gog, 1)
    back_outer(1, gog, 1)
    gather_forward("mg", gmg, 0, (0, 3))
    gather_own("mg", gmg, mg_piece, 1, (0, 3))
    reduce_y(1)
    hear_all()
    weights_core(0)
    rims_wait("x", xpad)
    act_rims(0, xpad)
    weights_wait(0)
    gather_wait("mg", gmg, 0)
    gather_forward("mg", gmg, 1, (1, 2))
    kernel_grad(0, gmg, 0)
    gather_forward("mg", gmg, 1, (0, 3))
    back_halos(0, gmg, 0)
    reduce_z(1)
    gather_wait("mg", gmg, 1)
    kernel_grad(0, gmg, 1)
    reduce_y(0)
    adam(1)
    back_halos(0, gmg, 1)
    back_inner(0, gmg, 0)
    back_outer(0, gmg, 0)
    back_inner(0, gmg, 1)
    reduce_z(0)
    spread_y(1)
    back_outer(0, gmg, 1)
    stores = [load(ig_buf, ig_out)]
    adam(0)
    stores += [load(adam_out.at[k], ref) for k, ref in enumerate((master_out, moment_out, second_out))]
    spread_y(0)
    spread_core(1)
    spread_wait(1)
    spread_core(0)
    spread_wait(0)
    for l in range(2):
        wait_in(new_kern.at[l], a_sem["store", l])
    for copy in stores:
        copy.wait()
    for copy, when in sends:
        if when is None:
            copy.wait_send()
        else:
            pl.when(when)(copy.wait_send)
    assert pool.used <= sems.shape[0], pool.used


def hand_over(ig, kern, master, moment, second, *refs):
    outs, held, sems = refs[:5], refs[5:10], refs[10]
    parts = [(1, (l, pl.ds(3 * r, 3))) for l in range(2) for r in range(3)]
    parts += [(0, (f,)) for f in range(2)] + [(k, (l,)) for k in (2, 3, 4) for l in range(2)]
    ins = (ig, kern, master, moment, second)
    steps = []
    for i, (k, at) in enumerate(parts):
        arrive = pltpu.make_async_copy(ins[k].at[at], held[k].at[at], sems.at[0, i])
        leave = pltpu.make_async_copy(held[k].at[at], outs[k].at[at], sems.at[1, i])
        arrive.start()
        steps.append((arrive, leave))
    for arrive, leave in steps:
        arrive.wait()
        leave.start()
    for arrive, leave in steps:
        leave.wait()


def on_device(section_input, middle, out_grad, kernels, master, moment, second):
    any_space = pl.BlockSpec(memory_space=pl.ANY)
    flat = lambda a: a.reshape(2, PX, 128)
    owned = lambda a: a.reshape(2, 9, 8, 128)
    state = jax.ShapeDtypeStruct((2, 9, 8, 128), F32)
    results = (
        jax.ShapeDtypeStruct((2, PX, 128), BF),
        jax.ShapeDtypeStruct((2, 9, 512, 128), BF),
        state, state, state,
    )
    outs = pl.pallas_call(
        kernel,
        out_shape=results,
        in_specs=[any_space] * 7,
        out_specs=[any_space] * 5,
        scratch_shapes=[
            pltpu.VMEM((2, PX + 256, 128), BF),
            pltpu.VMEM((2, PX + 256, 128), BF),
            pltpu.VMEM((2, PX + 256, 512), BF),
            pltpu.VMEM((2, PX + 256, 512), BF),
            pltpu.VMEM((2, 9, 128, 512), BF),
            pltpu.VMEM((2, 2, 384, PX + 256), BF),
            pltpu.VMEM((2, 4, 9, 128, 128), F32),
            pltpu.VMEM((512, 128), F32),
            pltpu.VMEM((2, 2, 2, 128, 128), F32),
            pltpu.VMEM((2, 2, 2, 128, 128), F32),
            pltpu.VMEM((2, 2, 9, 128, 128), F32),
            pltpu.VMEM((2, 4, 4, 2, SLAB, 128), BF),
            pltpu.VMEM((2, 3, 4, 2, SLAB, 128), BF),
            pltpu.VMEM((2, 4, 2, SLAB, 128), BF),
            pltpu.VMEM((2, 8, SLAB, 128), BF),
            pltpu.VMEM((3, 2, 9, 8, 128), F32),
            pltpu.VMEM((3, 2, 9, 8, 128), F32),
            pltpu.VMEM((2, 4, 16, SLAB, 128), BF),
            pltpu.VMEM((2, 9, 512, 128), BF),
            pltpu.VMEM((2, PX, 128), BF),
            pltpu.SemaphoreType.DMA((SEMS,)),
            pltpu.SemaphoreType.REGULAR((4,)),
        ],
        compiler_params=pltpu.CompilerParams(
            collective_id=0, has_side_effects=True, vmem_limit_bytes=VMEM_LIMIT
        ),
        cost_estimate=pl.CostEstimate(flops=10**10, bytes_accessed=10**7, transcendentals=10**6),
    )(
        flat(section_input), flat(middle), flat(out_grad),
        kernels.reshape(2, 9, 512, 128), owned(master), owned(moment), owned(second),
    )
    outs = pl.pallas_call(
        hand_over,
        out_shape=results,
        in_specs=[any_space] * 5,
        out_specs=[any_space] * 5,
        scratch_shapes=[pltpu.VMEM(r.shape, r.dtype) for r in results] + [pltpu.SemaphoreType.DMA((2, 14))],
    )(*outs)
    shapes = (section_input.shape, kernels.shape, master.shape, master.shape, master.shape)
    return tuple(out.reshape(shape) for out, shape in zip(outs, shapes))


def solution(mesh):
    activation = P("dp", None, "space", None, "chan")
    state = P(None, None, None, ("dp", "space"), "chan")
    weights = P(None, None, None, None, "chan")
    return jax.shard_map(
        on_device,
        mesh=mesh,
        in_specs=(activation, activation, activation, weights, state, state, state),
        out_specs=(activation, weights, state, state, state),
        check_vma=False,
    )
```

```python
import jax
import jax.numpy as jnp
from jax import lax
from jax.experimental import pallas as pl
from jax.experimental.pallas import tpu as pltpu
from jax.sharding import PartitionSpec as P

BF = jnp.bfloat16
F32 = jnp.float32
MESH = pl.DeviceIdType.MESH
PX = 1024
SLAB = 80
SEMS = 520
VMEM_LIMIT = 56 * 1024 * 1024


def sigmoid(v):
    return 1.0 / (1.0 + jnp.exp(-v))


def dsilu(v):
    sig = sigmoid(v)
    return sig * (1.0 + v * (1.0 - sig))


def nt_dot(a, b):
    return lax.dot_general(a, b, (((1,), (1,)), ((), ())), preferred_element_type=F32)


class Sems:
    def __init__(self, ref):
        self.ref = ref
        self.used = 0

    def take(self, count=1):
        base = self.used
        self.used += count
        return base


def kernel(
    x_in, mid_in, og_in, kern, master, moment, second,
    ig_out, kern_out, master_out, moment_out, second_out,
    xpad, midpad, gog, gmg, w, actt, red, back, halo_in, halo_out, core_in,
    ysend, yrecv, zsend, zrecv, adam_in, adam_out, slabs, new_kern, ig_buf, sems, meet,
):
    chan = lax.axis_index("chan")
    dp = lax.axis_index("dp")
    space = lax.axis_index("space")
    z_hi, core = dp // 2, dp % 2
    z_lo, y = space // 4, space % 4
    z = z_hi * 4 + z_lo
    pool = Sems(sems)
    sends = []

    def at_chan(p):
        return {"chan": (chan + p) % 4}

    def at_y(p):
        return {"space": z_lo * 4 + (y + p) % 4}

    def at_z_lo(p):
        return {"space": ((z_lo + p) % 4) * 4 + y}

    def at_z(p):
        other = (z + p) % 8
        return {"dp": (other // 4) * 2 + core, "space": (other % 4) * 4 + y}

    sibling = {"dp": z_hi * 2 + (1 - core)}
    has_prev = space > 0
    has_next = space < 15
    on_diagonal = chan == dp

    def send(src, dst, target, recv_sem, when=None):
        copy = pltpu.make_async_remote_copy(
            src_ref=src, dst_ref=dst, send_sem=sems.at[pool.take()], recv_sem=sems.at[recv_sem],
            device_id=target, device_id_type=MESH,
        )
        if when is None:
            copy.start()
        else:
            pl.when(when)(copy.start)
        sends.append((copy, when))

    def wait_in(dst, sem):
        pltpu.make_async_copy(dst, dst, sems.at[sem]).wait()

    def load(src, dst):
        copy = pltpu.make_async_copy(src, dst, sems.at[pool.take()])
        copy.start()
        return copy

    barrier = pltpu.get_barrier_semaphore()

    def signal(sem, target):
        pl.semaphore_signal(sem, inc=1, device_id=target, device_id_type=MESH)

    prev, nxt = {"space": space - 1}, {"space": space + 1}
    first_z, last_z = z_lo == 0, z_lo == 3
    for p in range(1, 4):
        signal(barrier, at_chan(p))
        signal(barrier, at_y(p))
        signal(barrier, at_z_lo(p))
    signal(barrier, sibling)
    pl.when(has_prev)(lambda: signal(barrier, prev))
    pl.when(has_next)(lambda: signal(barrier, nxt))
    pl.when(first_z)(lambda: signal(barrier, at_z(7)))

    inside = pl.ds(128, PX)
    load_mid = load(mid_in, midpad.at[:, inside, :])
    load_x = load(x_in, xpad.at[:, inside, :])
    load_og = load(og_in, gog.at[:, inside, pl.ds(0, 128)])
    w_parts = ((pl.ds(0, 6), y, at_y), (pl.ds(6, 3), z_lo, at_z_lo))

    def w_rows(index, core=core):
        return pl.ds(core * 64 + index * 16, 16)

    load_w = {
        (l, i): load(
            kern.at[l, taps, pl.ds(chan * 128 + core * 64 + index * 16, 16), :], w.at[l, taps, w_rows(index), pl.ds(0, 128)]
        )
        for l in (1, 0)
        for i, (taps, index, _) in enumerate(w_parts)
    }
    load_adam = [load(ref, adam_in.at[k]) for k, ref in enumerate((master, moment, second))]


    expected = 10 + has_prev.astype(jnp.int32) + has_next.astype(jnp.int32) + last_z.astype(jnp.int32)
    pl.semaphore_wait(barrier, expected)

    def hear_half():
        pl.when(last_z)(lambda: signal(meet.at[0], at_z(1)))

    def hear_ring():
        @pl.when(first_z)
        def _():
            pl.semaphore_wait(meet.at[0], 1)
            for p in range(1, 4):
                signal(meet.at[1], at_z_lo(p))

    def hear_sibling():
        pl.when(jnp.logical_not(first_z))(lambda: pl.semaphore_wait(meet.at[1], 1))
        signal(meet.at[2], sibling)

    def hear_chan():
        pl.semaphore_wait(meet.at[2], 1)
        for p in range(1, 4):
            signal(meet.at[3], at_chan(p))

    def hear_all():
        pl.semaphore_wait(meet.at[3], 3)

    def clear_edges():
        zero_row = jnp.zeros((128, 512), BF)
        for g in (gog, gmg):
            for f in range(2):
                g[f, pl.ds(0, 128), :] = zero_row
                g[f, pl.ds(128 + PX, 128), :] = zero_row

        @pl.when(space == 0)
        def _():
            for pad in (midpad, xpad):
                pad[:, pl.ds(0, 128), :] = jnp.zeros((2, 128, 128), BF)

        @pl.when(space == 15)
        def _():
            for pad in (midpad, xpad):
                pad[:, pl.ds(128 + PX, 128), :] = jnp.zeros((2, 128, 128), BF)

    gathers = {}

    pieces = range(4)

    def piece(f, i):
        return (f, pl.ds(128 + 256 * i, 256))

    def gather_own(name, g, src, f, order):
        sem = gathers.setdefault(name, {})
        for i in order:
            for k in ("left", "right", "far"):
                sem[k, f, i] = pool.take()
        for i, j in zip(order, tuple(order)[::-1]):
            send(src(f, i), g.at[(*piece(f, i), pl.ds(128, 128))], at_chan(1), sem["left", f, i])
            send(src(f, j), g.at[(*piece(f, j), pl.ds(384, 128))], at_chan(3), sem["right", f, j])

    def gather_forward(name, g, f, order):
        sem = gathers[name]
        for i in order:
            k, lanes, target = ("left", 128, at_chan(1)) if i < 2 else ("right", 384, at_chan(3))
            here = g.at[(*piece(f, i), pl.ds(lanes, 128))]
            wait_in(here, sem[k, f, i])
            send(here, g.at[(*piece(f, i), pl.ds(256, 128))], target, sem["far", f, i])

    def gather_wait(name, g, f):
        sem = gathers[name]
        for i in pieces:
            k, lanes = ("right", 384) if i < 2 else ("left", 128)
            wait_in(g.at[(*piece(f, i), pl.ds(lanes, 128))], sem[k, f, i])
            wait_in(g.at[(*piece(f, i), pl.ds(256, 128))], sem["far", f, i])

    w_sem = {}

    def weights_chan(l):
        for i, (taps, index, _) in enumerate(w_parts):
            for p in range(1, 4):
                w_sem["x", l, i, p] = pool.take()
                their = (chan + p) % 4
                send(
                    kern.at[l, taps, pl.ds(their * 128 + core * 64 + index * 16, 16), :],
                    w.at[l, taps, w_rows(index), pl.ds(128 * p, 128)],
                    at_chan(p), w_sem["x", l, i, p],
                )

    def weights_group(l):
        for i, (taps, index, at_peer) in enumerate(w_parts):
            load_w[l, i].wait()
            for p in range(1, 4):
                wait_in(w.at[l, taps, w_rows(index), pl.ds(128 * p, 128)], w_sem["x", l, i, p])
            here = w.at[l, taps, w_rows(index), :]
            for p in (2, 1, 3):
                w_sem["group", l, i, p] = pool.take()
                send(here, here, at_peer(p), w_sem["group", l, i, p])

    def weights_core(l):
        for p in (0, 1, 3, 2):
            for i, (taps, index, _) in enumerate(w_parts):
                here = w.at[l, taps, w_rows((index + 4 - p) % 4), :]
                if p:
                    wait_in(here, w_sem["group", l, i, p])
                w_sem["core", l, i, p] = pool.take()
                send(here, here, sibling, w_sem["core", l, i, p])

    def weights_wait(l):
        for p in (0, 1, 3, 2):
            for i, (taps, index, _) in enumerate(w_parts):
                wait_in(w.at[l, taps, w_rows((index + 4 - p) % 4, 1 - core), :], w_sem["core", l, i, p])

    rim_sem = {}

    def rims(k, src, pad):
        up, down = pool.take(), pool.take()
        rim_sem[k] = (up, down)
        send(src.at[:, pl.ds(PX - 128, 128), :], pad.at[:, pl.ds(0, 128), :], nxt, up, has_next)
        send(src.at[:, pl.ds(0, 128), :], pad.at[:, pl.ds(128 + PX, 128), :], prev, down, has_prev)

    def rims_wait(k, pad):
        up, down = rim_sem[k]
        pl.when(has_prev)(lambda: wait_in(pad.at[:, pl.ds(0, 128), :], up))
        pl.when(has_next)(lambda: wait_in(pad.at[:, pl.ds(128 + PX, 128), :], down))

    def transpose_act(l, pad, first, step, count):
        lane = lax.broadcasted_iota(jnp.int32, (128, 128), 1)

        def body(i, carry):
            f, row = i // count, first + step * (i % count)
            v = pad[f, pl.ds(pl.multiple_of(row * 128, 128), 128), :].astype(F32)
            a = (v * sigmoid(v)).astype(BF).astype(F32).T
            at = pl.ds(pl.multiple_of(row * 128, 128), 128)
            before = jnp.where(lane == 0, 0.0, pltpu.roll(a, 1, 1))
            after = jnp.where(lane == 127, 0.0, pltpu.roll(a, 127, 1))
            actt[l, f, pl.ds(0, 128), at] = before.astype(BF)
            actt[l, f, pl.ds(128, 128), at] = a.astype(BF)
            actt[l, f, pl.ds(256, 128), at] = after.astype(BF)
            return carry

        lax.fori_loop(0, 2 * count, body, 0)

    def act_inner(l, pad):
        transpose_act(l, pad, 1, 1, 8)

    def act_rims(l, pad):
        transpose_act(l, pad, 0, 9, 2)

    def kernel_grad(l, g, f):
        cotangent = g[f, inside, :]
        for r in range(3):
            part = jnp.dot(actt[l, f, :, pl.ds(128 * r, PX)], cotangent, preferred_element_type=F32)
            for k in range(4):
                block = part[:, 128 * k : 128 * k + 128].reshape(3, 128, 128)
                if f:
                    block = block + red[l, k, pl.ds(3 * r, 3)]
                red[l, k, pl.ds(3 * r, 3)] = block
            if f:
                reduce_core(l, r)

    def weight_rows(l, r):
        return w[l, pl.ds(3 * r, 3)].reshape(384, 512)

    def join_taps(acc):
        rows = acc.shape[0]
        col = lax.broadcasted_iota(jnp.int32, (rows, 128), 0) % 128
        first = jnp.where(col == 127, 0.0, pltpu.roll(acc[:, 0:128], rows - 1, 0))
        last = jnp.where(col == 0, 0.0, pltpu.roll(acc[:, 256:384], 1, 0))
        return first + acc[:, 128:256] + last

    halo_sem = {}

    def back_halos(l, g, f):
        up, down = pool.take(), pool.take()
        halo_sem[l, f] = (up, down)
        halo_out[l, f, 0] = join_taps(nt_dot(g[f, pl.ds(128, 128), :], weight_rows(l, 0)))
        halo_out[l, f, 1] = join_taps(nt_dot(g[f, pl.ds(PX, 128), :], weight_rows(l, 2)))
        send(halo_out.at[l, f, 0], halo_in.at[l, f, 1], prev, down, has_prev)
        send(halo_out.at[l, f, 1], halo_in.at[l, f, 0], nxt, up, has_next)

    def back_rows(l, g, f, i):
        start = i * 256
        acc = jnp.zeros((256, 384), F32)
        for r in range(3):
            rows = pl.ds(pl.multiple_of(start + (2 - r) * 128, 128), 256)
            acc = acc + nt_dot(g[f, rows, :], weight_rows(l, r))
        return join_taps(acc)

    def back_inner(l, g, f, first=1, end=3):
        def body(i, carry):
            finish(l, f, i * 256, back_rows(l, g, f, i))
            return carry

        lax.fori_loop(first, end, body, 0)

    def back_outer(l, g, f):
        def body(i, carry):
            back[pl.ds(pl.multiple_of(i * 256, 256), 256), :] = back_rows(l, g, f, i * 3)
            return carry

        lax.fori_loop(0, 2, body, 0)
        up, down = halo_sem[l, f]

        @pl.when(has_prev)
        def _():
            wait_in(halo_in.at[l, f, 0], up)
            back[pl.ds(0, 128), :] = back[pl.ds(0, 128), :] + halo_in[l, f, 0]

        @pl.when(has_next)
        def _():
            wait_in(halo_in.at[l, f, 1], down)
            back[pl.ds(384, 128), :] = back[pl.ds(384, 128), :] + halo_in[l, f, 1]

        def close(i, carry):
            finish(l, f, i * 768, back[pl.ds(pl.multiple_of(i * 256, 256), 256), :])
            return carry

        lax.fori_loop(0, 2, close, 0)

    def finish(l, f, start, total):
        rows = pl.ds(pl.multiple_of(start, 128), 256)
        padded = pl.ds(pl.multiple_of(start + 128, 128), 256)
        if l:
            v = midpad[f, padded, :].astype(F32)
            gmg[f, padded, pl.ds(0, 128)] = (total * dsilu(v)).astype(BF)
        else:
            v = xpad[f, padded, :].astype(F32)
            og = gog[f, padded, pl.ds(0, 128)].astype(F32)
            ig_buf[f, rows, :] = (og + total * dsilu(v)).astype(BF)

    r_sem = {}

    def slot_of(block):
        return (chan + 4 - block) % 4

    def reduce_core(l, r):
        for h in range(2):
            r_sem["core", l, h, r] = pool.take()
            taps = pl.ds(3 * r, 3)
            send(red.at[l, slot_of(2 * h + 1 - core), taps], core_in.at[l, h, taps], sibling, r_sem["core", l, h, r])

    def as_slab(v):
        return jnp.concatenate([v.reshape(72, 128), jnp.zeros((8, 128), F32)], axis=0).astype(BF)

    near_last = (2, 3, 1, 0)
    z_first = z_lo + 2 * ((chan // 2 + z_hi) % 2)

    def reduce_y(l):
        for r in range(3):
            for h in range(2):
                wait_in(core_in.at[l, h, pl.ds(3 * r, 3)], r_sem["core", l, h, r])
        for j in near_last:
            c = (z_first + j) % 4

            def body(q, carry, c=c):
                rows = pl.ds(pl.multiple_of(c * 32 + q * 8, 8), 8)
                for h in range(2):
                    total = red[l, slot_of(2 * h + core), :, rows, :] + core_in[l, h, :, rows, :]
                    ysend[l, q, c, h] = as_slab(total)
                return carry

            lax.fori_loop(0, 4, body, 0)
            for p in (2, 1, 3):
                r_sem["y", l, p, j] = pool.take()
                send(ysend.at[l, (y + p) % 4, c], yrecv.at[l, p - 1, j], at_y(p), r_sem["y", l, p, j])

    def reduce_z(l):
        r_sem["z", l] = pool.take(8)
        for j in near_last:
            c = (z_first + j) % 4
            for p in range(1, 4):
                wait_in(yrecv.at[l, p - 1, j], r_sem["y", l, p, j])
            for h in range(2):
                total = ysend[l, y, c, h].astype(F32)
                for p in range(3):
                    total = total + yrecv[l, p, j, h].astype(F32)
                total = total.astype(BF)
                zsend[l, j, h] = total
                owner = {"chan": 2 * h + core, "dp": chan, "space": c * 4 + y}
                mine = on_diagonal & (z_hi == h)
                away = jnp.logical_not(mine) if j == 0 else None
                send(zsend.at[l, j, h], zrecv.at[l, z], owner, r_sem["z", l] + z, away)
                if j == 0:

                    @pl.when(mine)
                    def _(total=total):
                        zrecv[l, z] = total

    a_sem = {}
    by_distance = (0, 1, 7, 2, 6, 3, 5, 4)

    def z_from(d):
        other = (z + 8 - d) % 8
        return (other // 4) * 2 + core, other % 4

    def adam(l):
        if l == 1:
            for copy in load_adam:
                copy.wait()
        for q in range(8):
            there = jnp.logical_not(on_diagonal & (z == q))
            pl.when(there)(lambda q=q: wait_in(zrecv.at[l, q], r_sem["z", l] + q))
        grads = zrecv[l, 0].astype(F32)
        for q in range(1, 8):
            grads = grads + zrecv[l, q].astype(F32)
        grads = grads[0:72].reshape(9, 8, 128)
        new_moment = 0.9 * adam_in[1, l] + 0.1 * grads
        new_second = 0.999 * adam_in[2, l] + 0.001 * grads * grads
        corrected = new_moment / (1.0 - 0.9**10)
        scale_term = jnp.sqrt(new_second / (1.0 - 0.999**10)) + 1e-08
        new_master = adam_in[0, l] - 0.01 * corrected / scale_term
        slabs[l, dp, space] = as_slab(new_master)
        here = slabs.at[l, dp, space]
        for p in by_distance[1:]:
            a_sem["z", l, p] = pool.take()
            send(here, here, at_z(p), a_sem["z", l, p])
        adam_out[0, l] = new_master
        adam_out[1, l] = new_moment
        adam_out[2, l] = new_second

    def to_y(l, d):
        dp_there, z_there = z_from(d)
        here = slabs.at[l, dp_there, z_there * 4 + y]
        for p in range(1, 4):
            a_sem["y", l, p, d] = pool.take()
            send(here, here, at_y(p), a_sem["y", l, p, d])

    def spread_y(l):
        for d in by_distance:
            if d:
                dp_there, z_there = z_from(d)
                wait_in(slabs.at[l, dp_there, z_there * 4 + y], a_sem["z", l, d])
            to_y(l, d)

    def assemble(l, dp_there, z_there):
        for pair in range(2):
            both = [
                slabs[l, dp_there, z_there * 4 + 2 * pair + i].astype(F32)[0:72].reshape(9, 8, 128) for i in range(2)
            ]
            rows = pl.ds(pl.multiple_of(dp_there * 128 + z_there * 32 + pair * 16, 16), 16)
            new_kern[l, :, rows, :] = jnp.concatenate(both, axis=1).astype(BF)
        rows = pl.ds(pl.multiple_of(dp_there * 128 + z_there * 32, 32), 32)
        pltpu.make_async_copy(new_kern.at[l, :, rows, :], kern_out.at[l, :, rows, :], sems.at[a_sem["store", l]]).start()

    def spread_core(l):
        a_sem["store", l] = pool.take()
        for d in by_distance:
            dp_there, z_there = z_from(d)
            for p in range(1, 4):
                wait_in(slabs.at[l, dp_there, z_there * 4 + (y + 4 - p) % 4], a_sem["y", l, p, d])
            a_sem["core", l, d] = pool.take()
            here = slabs.at[l, dp_there, pl.ds(z_there * 4, 4)]
            send(here, here, sibling, a_sem["core", l, d])
            assemble(l, dp_there, z_there)

    def spread_wait(l):
        for d in by_distance:
            dp_there, z_there = z_from(d)
            dp_there = dp_there + 1 - 2 * core
            wait_in(slabs.at[l, dp_there, pl.ds(z_there * 4, 4)], a_sem["core", l, d])
            assemble(l, dp_there, z_there)

    def og_piece(f, i):
        return og_in.at[f, pl.ds(256 * i, 256), :]

    def mg_piece(f, i):
        return gmg.at[(*piece(f, i), pl.ds(0, 128))]

    weights_chan(1)
    gather_own("og", gog, og_piece, 0, pieces)
    rims("mid", mid_in, midpad)
    weights_chan(0)
    hear_half()
    clear_edges()
    load_mid.wait()
    act_inner(1, midpad)
    weights_group(1)
    hear_ring()
    gather_forward("og", gog, 0, (0, 3, 1, 2))
    gather_own("og", gog, og_piece, 1, pieces)
    hear_sibling()
    rims_wait("mid", midpad)
    act_rims(1, midpad)
    weights_group(0)
    rims("x", x_in, xpad)
    load_x.wait()
    act_inner(0, xpad)
    gather_wait("og", gog, 0)
    load_og.wait()
    weights_core(1)
    hear_chan()
    kernel_grad(1, gog, 0)
    gather_forward("og", gog, 1, (0, 3, 1, 2))
    weights_wait(1)
    back_halos(1, gog, 0)
    back_inner(1, gog, 0, 1, 2)
    gather_own("mg", gmg, mg_piece, 0, (1,))
    back_inner(1, gog, 0, 2, 3)
    gather_own("mg", gmg, mg_piece, 0, (2,))
    back_outer(1, gog, 0)
    gather_own("mg", gmg, mg_piece, 0, (0, 3))
    gather_wait("og", gog, 1)
    back_halos(1, gog, 1)
    back_inner(1, gog, 1)
    gather_forward("mg", gmg, 0, (1, 2))
    gather_own("mg", gmg, mg_piece, 1, (1, 2))
    kernel_grad(1, gog, 1)
    back_outer(1, gog, 1)
    gather_forward("mg", gmg, 0, (0, 3))
    gather_own("mg", gmg, mg_piece, 1, (0, 3))
    reduce_y(1)
    hear_all()
    weights_core(0)
    rims_wait("x", xpad)
    act_rims(0, xpad)
    weights_wait(0)
    gather_wait("mg", gmg, 0)
    gather_forward("mg", gmg, 1, (1, 2))
    kernel_grad(0, gmg, 0)
    gather_forward("mg", gmg, 1, (0, 3))
    back_halos(0, gmg, 0)
    reduce_z(1)
    gather_wait("mg", gmg, 1)
    kernel_grad(0, gmg, 1)
    reduce_y(0)
    adam(1)
    back_halos(0, gmg, 1)
    back_inner(0, gmg, 0)
    back_outer(0, gmg, 0)
    back_inner(0, gmg, 1)
    reduce_z(0)
    spread_y(1)
    back_outer(0, gmg, 1)
    stores = [load(ig_buf, ig_out)]
    adam(0)
    stores += [load(adam_out.at[k], ref) for k, ref in enumerate((master_out, moment_out, second_out))]
    spread_y(0)
    spread_core(1)
    spread_wait(1)
    spread_core(0)
    spread_wait(0)
    for l in range(2):
        wait_in(new_kern.at[l], a_sem["store", l])
    for copy in stores:
        copy.wait()
    for copy, when in sends:
        if when is None:
            copy.wait_send()
        else:
            pl.when(when)(copy.wait_send)
    assert pool.used <= sems.shape[0], pool.used


def hand_over(ig, kern, master, moment, second, *refs):
    outs, held, sems = refs[:5], refs[5:10], refs[10]
    parts = [(1, (l, pl.ds(3 * r, 3))) for l in range(2) for r in range(3)]
    parts += [(0, (f,)) for f in range(2)] + [(k, (l,)) for k in (2, 3, 4) for l in range(2)]
    ins = (ig, kern, master, moment, second)
    steps = []
    for i, (k, at) in enumerate(parts):
        arrive = pltpu.make_async_copy(ins[k].at[at], held[k].at[at], sems.at[0, i])
        leave = pltpu.make_async_copy(held[k].at[at], outs[k].at[at], sems.at[1, i])
        arrive.start()
        steps.append((arrive, leave))
    for arrive, leave in steps:
        arrive.wait()
        leave.start()
    for arrive, leave in steps:
        leave.wait()


def on_device(section_input, middle, out_grad, kernels, master, moment, second):
    any_space = pl.BlockSpec(memory_space=pl.ANY)
    flat = lambda a: a.reshape(2, PX, 128)
    owned = lambda a: a.reshape(2, 9, 8, 128)
    state = jax.ShapeDtypeStruct((2, 9, 8, 128), F32)
    results = (
        jax.ShapeDtypeStruct((2, PX, 128), BF),
        jax.ShapeDtypeStruct((2, 9, 512, 128), BF),
        state, state, state,
    )
    outs = pl.pallas_call(
        kernel,
        out_shape=results,
        in_specs=[any_space] * 7,
        out_specs=[any_space] * 5,
        scratch_shapes=[
            pltpu.VMEM((2, PX + 256, 128), BF),
            pltpu.VMEM((2, PX + 256, 128), BF),
            pltpu.VMEM((2, PX + 256, 512), BF),
            pltpu.VMEM((2, PX + 256, 512), BF),
            pltpu.VMEM((2, 9, 128, 512), BF),
            pltpu.VMEM((2, 2, 384, PX + 256), BF),
            pltpu.VMEM((2, 4, 9, 128, 128), F32),
            pltpu.VMEM((512, 128), F32),
            pltpu.VMEM((2, 2, 2, 128, 128), F32),
            pltpu.VMEM((2, 2, 2, 128, 128), F32),
            pltpu.VMEM((2, 2, 9, 128, 128), F32),
            pltpu.VMEM((2, 4, 4, 2, SLAB, 128), BF),
            pltpu.VMEM((2, 3, 4, 2, SLAB, 128), BF),
            pltpu.VMEM((2, 4, 2, SLAB, 128), BF),
            pltpu.VMEM((2, 8, SLAB, 128), BF),
            pltpu.VMEM((3, 2, 9, 8, 128), F32),
            pltpu.VMEM((3, 2, 9, 8, 128), F32),
            pltpu.VMEM((2, 4, 16, SLAB, 128), BF),
            pltpu.VMEM((2, 9, 512, 128), BF),
            pltpu.VMEM((2, PX, 128), BF),
            pltpu.SemaphoreType.DMA((SEMS,)),
            pltpu.SemaphoreType.REGULAR((4,)),
        ],
        compiler_params=pltpu.CompilerParams(
            collective_id=0, has_side_effects=True, vmem_limit_bytes=VMEM_LIMIT
        ),
        cost_estimate=pl.CostEstimate(flops=10**10, bytes_accessed=10**7, transcendentals=10**6),
    )(
        flat(section_input), flat(middle), flat(out_grad),
        kernels.reshape(2, 9, 512, 128), owned(master), owned(moment), owned(second),
    )
    outs = pl.pallas_call(
        hand_over,
        out_shape=results,
        in_specs=[any_space] * 5,
        out_specs=[any_space] * 5,
        scratch_shapes=[pltpu.VMEM(r.shape, r.dtype) for r in results] + [pltpu.SemaphoreType.DMA((2, 14))],
    )(*outs)
    shapes = (section_input.shape, kernels.shape, master.shape, master.shape, master.shape)
    return tuple(out.reshape(shape) for out, shape in zip(outs, shapes))


def solution(mesh):
    activation = P("dp", None, "space", None, "chan")
    state = P(None, None, None, ("dp", "space"), "chan")
    weights = P(None, None, None, None, "chan")
    return jax.shard_map(
        on_device,
        mesh=mesh,
        in_specs=(activation, activation, activation, weights, state, state, state),
        out_specs=(activation, weights, state, state, state),
        check_vma=False,
    )
```
